512 devices in a mesh: resp: 16 (over x_lo, y, core), ctx: 32 (over z, x_hi).
Axes of the slice: x: 4 (x_hi: 2, x_lo: 2; x = x_hi * 2 + x_lo), y: 4, z: 16, core: 2. Of those that a mesh axis runs over, the one named last changes fastest.
Arguments:
- queries: bfloat16 [32, 2048, 8, 128], P('resp', 'ctx'), may hold values from -170 to 170
- prompt_keys: bfloat16 [512, 128], P('ctx'), may hold values from -6 to 6
- prompt_values: bfloat16 [512, 128], P('ctx'), may hold values from -6 to 6
- resp_keys: bfloat16 [32, 2048, 128], P('resp', 'ctx'), may hold values from -6 to 6
- resp_values: bfloat16 [32, 2048, 128], P('resp', 'ctx'), may hold values from -6 to 6
- upstream: bfloat16 [32, 2048, 8, 128], P('resp', 'ctx'), may hold values from -6 to 6
- behav_logp: float32 [32, 2048], P('resp', 'ctx'), may hold values from -2.5 to -0.1
- cur_logp: float32 [32, 2048], P('resp', 'ctx'), may hold values from -2.5 to -0.1
- advantages: float32 [32], P('resp'), may hold values from -4 to 4
- lengths: int32 [32], P('resp'), may hold values from 128 to 2048, as said below
Outputs:
- grad_queries: bfloat16 [32, 2048, 8, 128], P('resp', 'ctx')
- grad_resp_keys: bfloat16 [32, 2048, 128], P('resp', 'ctx')
- grad_resp_values: bfloat16 [32, 2048, 128], P('resp', 'ctx')
- grad_prompt_keys: float32 [512, 128], P('ctx')
- grad_prompt_values: float32 [512, 128], P('ctx')
The draws below stay inside these ranges and needn't reach their ends.
Inputs may be any that keep to these rules, and one draw needn't show every extreme that they name: `lengths`: each length is a multiple of 128; in every draw one response has length 2048 and another has length 128.
All inputs are finite; a program needn't handle non-finite values.
Results may differ from the reference program's by a relative error of at most 0.024.
Values may be sent and summed in bfloat16 or wider, within the bound.
A program may use at most 64 MiB of HBM per device.

```python
import jax
import jax.numpy as jnp
from jax import lax

HD = 128
H = 8
L = 2048
BLK = 128
PCTX = 16
P_SIZE = 512
R = 32
N_CTX = 32


def prompt_rows(key):
    base = jnp.clip(jax.random.normal(key, (P_SIZE, HD), jnp.float32), -6.0, 6.0)
    paired = (jnp.arange(P_SIZE, dtype=jnp.int32) % PCTX == 1)[:, None]
    return jnp.where(paired, base, base)


def draw_prompt_keys(key, part):
    rows = prompt_rows(key)
    return rows.astype(jnp.bfloat16)


def draw_queries(key, part):
    key = jax.random.fold_in(key, 7)
    drawn = jnp.clip(jax.random.normal(key, (R, L, H, HD), jnp.float32), -6.0, 6.0)
    return drawn.astype(jnp.bfloat16)


def draw_lengths(key, part):
    key = jax.random.fold_in(key, 3)
    blocks = jax.random.randint(jax.random.fold_in(key, 1), (R,), 1, L // BLK + 1)
    longest = jax.random.randint(jax.random.fold_in(key, 2), (), 0, R)
    shortest = (longest + jax.random.randint(jax.random.fold_in(key, 4), (), 1, R)) % R
    member_ids = jnp.arange(R, dtype=jnp.int32)
    blocks = jnp.where(member_ids == longest, L // BLK, jnp.where(member_ids == shortest, 1, blocks))
    return (blocks * BLK).astype(jnp.int32)


def shard_levels(stream_key, dims, split, low, top_value):
    factor_of, own = 1.0, jax.random.fold_in(stream_key, 6)
    for dim, shards_of in split:
        draws = jnp.exp(jax.random.uniform(jax.random.fold_in(own, dim), (shards_of,), jnp.float32, low / len(split), top_value / len(split)))
        factor_of = factor_of * jnp.repeat(draws, dims[dim] // shards_of).reshape([-1 if axis == dim else 1 for axis in range(len(dims))])
    return factor_of


def bell_draw(stream_key, shape, scale, most, cuts=(), kind=jnp.bfloat16):
    factor_of = shard_levels(stream_key, shape, cuts, -0.22, 0.18) if cuts else 1.0
    array = jax.random.normal(stream_key, shape, jnp.float32) * scale * factor_of
    return jnp.minimum(jnp.maximum(array, -most), most).astype(kind)


def setup_inputs(seed: int = 0) -> dict:
    seeds = jax.random.split(jax.random.key(seed), 11)
    queries = draw_queries(jax.random.fold_in(seeds[10], 71), 0)
    prompt_keys = draw_prompt_keys(jax.random.fold_in(seeds[10], 71), 0)
    prompt_values = bell_draw(seeds[2], (P_SIZE, HD), 1.0, 6.0, ((0, 32),))
    resp_keys = bell_draw(seeds[3], (R, L, HD), 1.0, 6.0, ((0, 16), (1, 32)))
    resp_values = bell_draw(seeds[4], (R, L, HD), 1.0, 6.0, ((0, 16), (1, 32)))
    upstream = bell_draw(seeds[5], (R, L, H, HD), 1.0, 6.0, ((0, 16), (1, 32)))
    behav_logp = jnp.clip(-2.5 + 2.4 * jax.random.uniform(seeds[6], (R, L), jnp.float32) ** shard_levels(seeds[6], (R, L), ((0, 16), (1, 32)), -0.2, 0.2), -2.5, -0.1)
    cur_logp = jnp.clip(-2.5 + 2.4 * jax.random.uniform(seeds[7], (R, L), jnp.float32) ** shard_levels(seeds[7], (R, L), ((0, 16), (1, 32)), -0.2, 0.2), -2.5, -0.1)
    advantages = bell_draw(seeds[8], (R,), 1.0, 4.0, ((0, 16),), jnp.float32)
    lengths = draw_lengths(jax.random.fold_in(seeds[10], 71), 0)
    return dict(queries=queries, prompt_keys=prompt_keys, prompt_values=prompt_values, resp_keys=resp_keys, resp_values=resp_values, upstream=upstream, behav_logp=behav_logp, cur_logp=cur_logp, advantages=advantages, lengths=lengths)


RATIO_CAP = 2.0


def token_weights(advantages, behav_logp, cur_logp, lengths, positions, full_len):
    ratio = jnp.minimum(jnp.exp(cur_logp - behav_logp), RATIO_CAP)
    valid = (positions[None, :] < lengths[:, None]).astype(jnp.float32)
    spread = full_len / lengths.astype(jnp.float32)
    return -advantages[:, None] * ratio * valid * spread[:, None]


def attend_block(query_rows, grad_rows, keys_all, values_all, row_pos, col_pos, softmax_scale):
    scores = jnp.dot(query_rows, keys_all.T, preferred_element_type=jnp.float32) * softmax_scale
    scores = jnp.where(col_pos[None, :] <= row_pos[:, None], scores, -jnp.inf)
    row_max = jnp.max(scores, axis=1, keepdims=True)
    shifted = jnp.exp(scores - row_max)
    probs = lax.optimization_barrier((shifted / jnp.sum(shifted, axis=1, keepdims=True)).astype(jnp.bfloat16))
    attended = lax.optimization_barrier(jnp.dot(probs, values_all, preferred_element_type=jnp.float32).astype(jnp.bfloat16))
    deltas = jnp.sum(grad_rows.astype(jnp.float32) * attended.astype(jnp.float32), axis=1)
    grad_probs = jnp.dot(grad_rows, values_all.T, preferred_element_type=jnp.float32)
    grad_scores = (probs.astype(jnp.float32) * (grad_probs - deltas[:, None])).astype(jnp.bfloat16)
    query_grad = (jnp.dot(grad_scores, keys_all, preferred_element_type=jnp.float32) * softmax_scale).astype(jnp.bfloat16)
    return probs, grad_scores, query_grad


def reference(queries, prompt_keys, prompt_values, resp_keys, resp_values, upstream, behav_logp, cur_logp, advantages, lengths):
    block_len = L // N_CTX
    softmax_scale = HD ** -0.5
    positions = jnp.arange(L, dtype=jnp.int32)
    weights = token_weights(advantages, behav_logp, cur_logp, lengths, positions, L)
    grad_out = (weights[:, :, None, None] * upstream.astype(jnp.float32)).astype(jnp.bfloat16)
    col_pos = jnp.concatenate([jnp.full((P_SIZE,), -1, jnp.int32), positions])
    head_pos = jnp.repeat(jnp.arange(block_len, dtype=jnp.int32), H)

    def per_response(prompt_acc, inputs):
        query_all, grad_all, keys_resp, values_resp = inputs
        keys_all = jnp.concatenate([prompt_keys, keys_resp], 0)
        values_all = jnp.concatenate([prompt_values, values_resp], 0)
        query_blocks = query_all.reshape(N_CTX, block_len * H, HD)
        grad_blocks = grad_all.reshape(N_CTX, block_len * H, HD)

        def per_block(carry, block_inputs):
            prompt_sum, resp_sum = carry
            block_index, query_rows, grad_rows = block_inputs
            row_pos = block_index * block_len + head_pos
            probs, grad_scores, query_grad = attend_block(query_rows, grad_rows, keys_all, values_all, row_pos, col_pos, softmax_scale)
            key_grad = jnp.dot(grad_scores.T, query_rows, preferred_element_type=jnp.float32) * softmax_scale
            value_grad = jnp.dot(probs.T, grad_rows, preferred_element_type=jnp.float32)
            prompt_sum = prompt_sum + jnp.concatenate([key_grad[:P_SIZE], value_grad[:P_SIZE]], 1)
            resp_part = lax.optimization_barrier(jnp.concatenate([key_grad[P_SIZE:], value_grad[P_SIZE:]], 1).astype(jnp.bfloat16))
            resp_sum = resp_sum + resp_part.astype(jnp.float32)
            return (prompt_sum, resp_sum), query_grad

        start_resp = jnp.zeros((L, 2 * HD), jnp.float32)
        (prompt_acc, resp_sum), query_grads = lax.scan(per_block, (prompt_acc, start_resp), (jnp.arange(N_CTX, dtype=jnp.int32), query_blocks, grad_blocks))
        return prompt_acc, (query_grads.reshape(L, H, HD), resp_sum.astype(jnp.bfloat16))

    start_prompt = jnp.zeros((P_SIZE, 2 * HD), jnp.float32)
    prompt_total, (grad_queries, resp_grads) = lax.scan(per_response, start_prompt, (queries, grad_out, resp_keys, resp_values))
    return grad_queries, resp_grads[:, :, :HD], resp_grads[:, :, HD:], prompt_total[:, :HD], prompt_total[:, HD:]
```

```python
import functools

import jax
import jax.numpy as jnp
from jax import lax
from jax.experimental import pallas as pl
from jax.experimental.pallas import tpu as pltpu
from jax.sharding import PartitionSpec as P

RATIO_CAP = 2.0
MESH = pl.DeviceIdType.MESH
F32 = jnp.float32
BF16 = jnp.bfloat16


def kernel(
    q_ref, u_ref, pk_ref, pv_ref, rk_ref, rv_ref, behav_ref, cur_ref, adv_ref, len_ref,
    gq_ref, grk_ref, grv_ref, gpk_ref, gpv_ref,
    kv, xkv, qb, gb, gsend, qt, gt, sc, dp, mx, sm, dl, dqt, pp, part, first, rs, fin, xfin, dqs, pself, pother, pr,
    ag_s, ag_r, rs_s, rs_r, x_s, x_r, p_s, p_r,
    *, nz, nr, tok, heads, prow, full_len,
):
    hd = q_ref.shape[-1]
    scale = hd ** (-0.5)
    half = nz // 2
    rows = tok * heads
    two = 2 * rows
    key_rows = 2 * tok
    n_resp_chunks = nz
    p_chunks = (2 * nz * prow) // key_rows
    per_chunk = key_rows // (2 * prow)

    c = lax.axis_index("ctx")
    r = lax.axis_index("resp")
    z = c // 2
    h = c % 2
    g = 1 - h
    partner = {"ctx": 2 * z + g}
    up = {"ctx": 2 * ((z + 1) % nz) + h}
    down = {"ctx": 2 * ((z + nz - 1) % nz) + h}
    ring_to = (up, down)

    barrier = pltpu.get_barrier_semaphore()
    for dev in (partner, up, down):
        pl.semaphore_signal(barrier, 1, device_id=dev, device_id_type=MESH)
    for d in range(1, nr):
        pl.semaphore_signal(barrier, 1, device_id={"resp": (r + d) % nr}, device_id_type=MESH)

    k_at, v_at, pk_at, pv_at = 0, tok, 2 * tok, 2 * tok + prow
    kv[z, h, pl.ds(k_at, tok)] = rk_ref[h]
    kv[z, h, pl.ds(v_at, tok)] = rv_ref[h]
    kv[z, h, pl.ds(pk_at, prow)] = pk_ref[...]
    kv[z, h, pl.ds(pv_at, prow)] = pv_ref[...]
    xkv[pl.ds(k_at, tok)] = rk_ref[g]
    xkv[pl.ds(v_at, tok)] = rv_ref[g]
    xkv[pl.ds(pk_at, prow)] = pk_ref[...]
    xkv[pl.ds(pv_at, prow)] = pv_ref[...]

    def remote(src, dst, ssem, rsem, dev):
        return pltpu.make_async_remote_copy(
            src_ref=src, dst_ref=dst, send_sem=ssem, recv_sem=rsem, device_id=dev, device_id_type=MESH
        )

    x_kv = remote(xkv, kv.at[z, h], x_s.at[0], x_r.at[0], partner)
    x_kv_in = remote(xkv, kv.at[z, g], x_s.at[0], x_r.at[0], partner)
    x_q = remote(q_ref.at[g], qb.at[h], x_s.at[1], x_r.at[1], partner)
    x_q_in = remote(q_ref.at[g], qb.at[g], x_s.at[1], x_r.at[1], partner)
    x_g = remote(gsend, gb.at[h], x_s.at[2], x_r.at[2], partner)
    x_g_in = remote(gsend, gb.at[g], x_s.at[2], x_r.at[2], partner)

    def ag_copy(d, s, blk):
        chunk = (z - s + nz) % nz if d == 0 else (z + s) % nz
        return remote(kv.at[chunk, blk], kv.at[chunk, blk], ag_s.at[d, s, blk], ag_r.at[d, s, blk], ring_to[d])

    def ag_recv(d, s, blk):
        chunk = (z - 1 - s + 2 * nz) % nz if d == 0 else (z + 1 + s) % nz
        return remote(kv.at[chunk, blk], kv.at[chunk, blk], ag_s.at[d, s, blk], ag_r.at[d, s, blk], ring_to[d])

    pl.semaphore_wait(barrier, 2 + nr)
    x_kv.start()
    for d in range(2):
        ag_copy(d, 0, h).start()
    x_q.start()

    row_of = lax.broadcasted_iota(jnp.int32, (rows, tok), 0) // heads
    col_of = lax.broadcasted_iota(jnp.int32, (rows, tok), 1)
    position = c * tok + lax.broadcasted_iota(jnp.int32, (1, tok), 1)

    def weighted(member):
        length = jnp.full((1, tok), len_ref[member], jnp.int32)
        ratio = jnp.minimum(jnp.exp(cur_ref[pl.ds(member, 1), :] - behav_ref[pl.ds(member, 1), :]), RATIO_CAP)
        valid = (position < length).astype(F32)
        weight = -adv_ref[member] * ratio * valid * (full_len / length.astype(F32))
        spread = jnp.where(row_of == col_of, jnp.broadcast_to(weight, (rows, tok)), 0.0)
        column = jnp.sum(spread, axis=1, keepdims=True)
        return (column * u_ref[member].astype(F32)).astype(BF16)

    gsend[...] = weighted(g)
    x_g.start()
    gb[h] = weighted(h)
    qb[h] = q_ref[h]

    x_kv_in.wait_recv()
    for d in range(2):
        ag_copy(d, 0, g).start()
    x_q_in.wait_recv()
    qt[...] = qb[...].reshape(two, hd).T
    x_g_in.wait_recv()
    gt[...] = gb[...].reshape(two, hd).T

    def scores_of(keys, values):
        s = jnp.dot(keys, qt[...], preferred_element_type=F32) * scale
        return s, jnp.dot(values, gt[...], preferred_element_type=F32)

    def chunk_of(j, at):
        return kv[j, :, pl.ds(at, tok), :].reshape(key_rows, hd)

    def prompt_of(i, at):
        return kv[pl.ds(i * per_chunk, per_chunk), :, pl.ds(at, prow), :].reshape(key_rows, hd)

    s, grad_p = scores_of(chunk_of(z, k_at), chunk_of(z, v_at))
    key_pos = lax.broadcasted_iota(jnp.int32, (key_rows, two), 0)
    row_pos = lax.broadcasted_iota(jnp.int32, (key_rows, two), 1) // heads
    s = jnp.where(key_pos <= row_pos, s, -jnp.inf)
    sc[z] = s
    dp[z] = grad_p
    m = jnp.max(s, axis=0, keepdims=True)
    e = jnp.exp(s - m)
    mx[...] = m
    sm[...] = jnp.sum(e, axis=0, keepdims=True)
    dl[...] = jnp.sum(e * grad_p, axis=0, keepdims=True)

    def take(j, keys, values):
        s, grad_p = scores_of(keys, values)
        sc[j] = s
        dp[j] = grad_p
        old = mx[...]
        m = jnp.maximum(old, jnp.max(s, axis=0, keepdims=True))
        e = jnp.exp(s - m)
        fix = jnp.exp(old - m)
        mx[...] = m
        sm[...] = sm[...] * fix + jnp.sum(e, axis=0, keepdims=True)
        dl[...] = dl[...] * fix + jnp.sum(e * grad_p, axis=0, keepdims=True)

    def take_chunk(j):
        @pl.when(j < z)
        def _():
            take(j, chunk_of(j, k_at), chunk_of(j, v_at))

    def ag_step(s, _):
        for blk in (h, g):
            ag_recv(0, s - 1, blk).wait_recv()
            ag_copy(0, s, blk).start()
            ag_recv(1, s - 1, blk).wait_recv()

            @pl.when(s < half - 1)
            def _():
                ag_copy(1, s, blk).start()

        take_chunk((z - s + nz) % nz)
        take_chunk((z + s) % nz)
        return 0

    lax.fori_loop(1, half, ag_step, 0)
    for blk in range(2):
        ag_recv(0, half - 1, blk).wait_recv()
    take_chunk((z + half) % nz)

    def take_prompt(i, _):
        take(n_resp_chunks + i, prompt_of(i, pk_at), prompt_of(i, pv_at))
        return 0

    lax.fori_loop(0, p_chunks, take_prompt, 0)

    inv = 1.0 / sm[...]
    sm[...] = inv
    dl[...] = dl[...] * inv
    dqt[...] = jnp.zeros_like(dqt)

    def give(j, keys):
        probs = (jnp.exp(sc[j] - mx[...]) * sm[...]).astype(BF16)
        grad_s = (probs.astype(F32) * (dp[j] - dl[...])).astype(BF16)
        d_values = jnp.dot(probs, gb[...].reshape(two, hd), preferred_element_type=F32)
        d_keys = jnp.dot(grad_s, qb[...].reshape(two, hd), preferred_element_type=F32) * scale
        dqt[...] += jnp.dot(keys.T, grad_s, preferred_element_type=F32)
        return d_keys.astype(BF16), d_values.astype(BF16)

    def give_prompt(i, _):
        d_keys, d_values = give(n_resp_chunks + i, prompt_of(i, pk_at))
        pp[pl.ds(i * per_chunk, per_chunk), :, pl.ds(0, prow), :] = d_keys.reshape(per_chunk, 2, prow, hd)
        pp[pl.ds(i * per_chunk, per_chunk), :, pl.ds(prow, prow), :] = d_values.reshape(per_chunk, 2, prow, hd)
        return 0

    lax.fori_loop(0, p_chunks, give_prompt, 0)

    def rs_chunk(d, s):
        return (z + half - s + nz) % nz if d == 0 else (z + half + 1 + s) % nz

    def give_chunk(j, dst):
        @pl.when(j <= z)
        def _():
            d_keys, d_values = give(j, chunk_of(j, k_at))
            dst[:, pl.ds(k_at, tok), :] = d_keys.reshape(2, tok, hd)
            dst[:, pl.ds(v_at, tok), :] = d_values.reshape(2, tok, hd)

        @pl.when(j > z)
        def _():
            dst[:, pl.ds(0, 2 * tok), :] = jnp.zeros((2, 2 * tok, hd), BF16)

        dst[:, pl.ds(pk_at, 2 * prow), :] = pp[j]

    def rs_first(d, blk):
        return remote(first.at[d, blk], rs.at[d, 0, blk], rs_s.at[d, 0, blk], rs_r.at[d, 0, blk], ring_to[d])

    def rs_in(d, s, blk):
        return remote(rs.at[d, s, blk], rs.at[d, s, blk], rs_s.at[d, s, blk], rs_r.at[d, s, blk], ring_to[d])

    def rs_next(d, s, blk):
        return remote(rs.at[d, s - 1, blk], rs.at[d, s, blk], rs_s.at[d, s, blk], rs_r.at[d, s, blk], ring_to[d])

    for d in range(2):
        give_chunk(rs_chunk(d, 0), first.at[d])
        for blk in range(2):
            rs_first(d, blk).start()
    for d in range(2):
        give_chunk(rs_chunk(d, 1), part.at[1, d])

    def rs_step(s, _):
        slot = s % 2
        for d in range(2):
            for blk in range(2):
                rs_in(d, s - 1, blk).wait_recv()
                total = rs[d, s - 1, blk].astype(F32) + part[slot, d, blk].astype(F32)
                rs[d, s - 1, blk] = total.astype(BF16)
                rs_next(d, s, blk).start()

        for d in range(2):
            give_chunk(rs_chunk(d, s + 1), part.at[1 - slot, d])
        return 0

    lax.fori_loop(1, half - 1, rs_step, 0)

    last = (half - 1) % 2
    d_q = (dqt[...] * scale).T.astype(BF16).reshape(2, rows, hd)
    dqs[...] = d_q
    gq_ref[h] = dqs[h]
    x_dq = remote(dqs.at[g], gq_ref.at[h], x_s.at[3], x_r.at[3], partner)
    x_dq_in = remote(dqs.at[g], gq_ref.at[g], x_s.at[3], x_r.at[3], partner)
    x_dq.start()

    for blk in range(2):
        rs_in(0, half - 2, blk).wait_recv()
        total = rs[0, half - 2, blk].astype(F32) + part[last, 0, blk].astype(F32)
        rs[0, half - 2, blk] = total.astype(BF16)
        rs_next(0, half - 1, blk).start()
    for blk in range(2):
        rs_in(1, half - 2, blk).wait_recv()
    for blk in range(2):
        rs_in(0, half - 1, blk).wait_recv()

    def final(blk):
        return (
            part[last, 1, blk].astype(F32) + rs[1, half - 2, blk].astype(F32) + rs[0, half - 1, blk].astype(F32)
        )

    other = final(g)
    fin[...] = other[: 2 * tok].astype(BF16)
    pother[...] = other[2 * tok :]
    x_p = remote(pother, pself.at[h], x_s.at[4], x_r.at[4], partner)
    x_p_in = remote(pother, pself.at[g], x_s.at[4], x_r.at[4], partner)
    x_p.start()
    x_f = remote(fin, xfin, x_s.at[5], x_r.at[5], partner)
    x_f.start()
    mine = final(h)
    grk_ref[h] = mine[:tok].astype(BF16)
    grv_ref[h] = mine[tok : 2 * tok].astype(BF16)
    pself[h] = mine[2 * tok :]
    x_p_in.wait_recv()
    pr[r] = pself[0] + pself[1]

    def p_copy(d):
        return remote(pr.at[r], pr.at[r], p_s.at[d], p_r.at[r], {"resp": (r + d) % nr})

    def p_in(d):
        src = (r + d) % nr
        return remote(pr.at[src], pr.at[src], p_s.at[d], p_r.at[src], {"resp": src})

    for d in range(1, nr):
        p_copy(d).start()
    x_f.wait_recv()
    grk_ref[g] = xfin[pl.ds(0, tok)]
    grv_ref[g] = xfin[pl.ds(tok, tok)]
    x_dq_in.wait_recv()
    for d in range(1, nr):
        p_in(d).wait_recv()
    total = pr[0]
    for i in range(1, nr):
        total = total + pr[i]
    gpk_ref[...] = total[:prow]
    gpv_ref[...] = total[prow:]

    for item in (x_kv, x_q, x_g, x_dq, x_p, x_f):
        item.wait_send()
    for d in range(1, nr):
        p_copy(d).wait_send()
    for d in range(2):
        for s in range(half if d == 0 else half - 1):
            for blk in range(2):
                ag_copy(d, s, blk).wait_send()
                rs_in(d, s, blk).wait_send()


def per_device(queries, prompt_keys, prompt_values, resp_keys, resp_values, upstream, behav_logp, cur_logp, advantages, lengths):
    members, tok, heads, hd = queries.shape
    nc = lax.axis_size("ctx")
    nr = lax.axis_size("resp")
    nz = nc // 2
    half = nz // 2
    prow = prompt_keys.shape[0]
    rows = tok * heads
    two = 2 * rows
    key_rows = 2 * tok
    blk = 2 * tok + 2 * prow
    slots = nz + (nc * prow) // key_rows
    vmem = pl.BlockSpec(memory_space=pltpu.VMEM)
    smem = pl.BlockSpec(memory_space=pltpu.SMEM)
    dma = pltpu.SemaphoreType.DMA
    outs = pl.pallas_call(
        functools.partial(kernel, nz=nz, nr=nr, tok=tok, heads=heads, prow=prow, full_len=tok * nc),
        name="grpo_backward",
        out_shape=(
            jax.ShapeDtypeStruct((members, rows, hd), BF16),
            jax.ShapeDtypeStruct((members, tok, hd), BF16),
            jax.ShapeDtypeStruct((members, tok, hd), BF16),
            jax.ShapeDtypeStruct((prow, hd), F32),
            jax.ShapeDtypeStruct((prow, hd), F32),
        ),
        in_specs=[vmem] * 8 + [smem] * 2,
        out_specs=(vmem,) * 5,
        scratch_shapes=[
            pltpu.VMEM((nz, 2, blk, hd), BF16),
            pltpu.VMEM((blk, hd), BF16),
            pltpu.VMEM((2, rows, hd), BF16),
            pltpu.VMEM((2, rows, hd), BF16),
            pltpu.VMEM((rows, hd), BF16),
            pltpu.VMEM((hd, two), BF16),
            pltpu.VMEM((hd, two), BF16),
            pltpu.VMEM((slots, key_rows, two), F32),
            pltpu.VMEM((slots, key_rows, two), F32),
            pltpu.VMEM((1, two), F32),
            pltpu.VMEM((1, two), F32),
            pltpu.VMEM((1, two), F32),
            pltpu.VMEM((hd, two), F32),
            pltpu.VMEM((nz, 2, 2 * prow, hd), BF16),
            pltpu.VMEM((2, 2, 2, blk, hd), BF16),
            pltpu.VMEM((2, 2, blk, hd), BF16),
            pltpu.VMEM((2, half, 2, blk, hd), BF16),
            pltpu.VMEM((2 * tok, hd), BF16),
            pltpu.VMEM((2 * tok, hd), BF16),
            pltpu.VMEM((2, rows, hd), BF16),
            pltpu.VMEM((2, 2 * prow, hd), F32),
            pltpu.VMEM((2 * prow, hd), F32),
            pltpu.VMEM((nr, 2 * prow, hd), F32),
            dma((2, half, 2)),
            dma((2, half, 2)),
            dma((2, half, 2)),
            dma((2, half, 2)),
            dma((6,)),
            dma((6,)),
            dma((nr,)),
            dma((nr,)),
        ],
        compiler_params=pltpu.CompilerParams(
            collective_id=0, has_side_effects=True, vmem_limit_bytes=48 * 1024 * 1024
        ),
    )(
        queries.reshape(members, rows, hd),
        upstream.reshape(members, rows, hd),
        prompt_keys, prompt_values, resp_keys, resp_values, behav_logp, cur_logp, advantages, lengths,
    )
    return (outs[0].reshape(queries.shape), *outs[1:])


def solution(mesh):
    placed = (
        P("resp", "ctx", None, None),
        P("ctx", None),
        P("ctx", None),
        P("resp", "ctx", None),
        P("resp", "ctx", None),
        P("resp", "ctx", None, None),
        P("resp", "ctx"),
        P("resp", "ctx"),
        P("resp"),
        P("resp"),
    )
    return jax.shard_map(
        per_device,
        mesh=mesh,
        in_specs=placed,
        out_specs=(
            P("resp", "ctx", None, None),
            P("resp", "ctx", None),
            P("resp", "ctx", None),
            P("ctx", None),
            P("ctx", None),
        ),
        check_vma=False,
    )
```

```python
import functools

import jax
import jax.numpy as jnp
from jax import lax
from jax.experimental import pallas as pl
from jax.experimental.pallas import tpu as pltpu
from jax.sharding import PartitionSpec as P

RATIO_CAP = 2.0
MESH = pl.DeviceIdType.MESH
F32 = jnp.float32
BF16 = jnp.bfloat16
LAST = (8, 7)
ORDER = (1, 4, 2, 5, 7, 3, 6, 8)
PARENT = {1: 0, 2: 1, 3: 2, 4: 0, 5: 4, 6: 5, 7: 4, 8: 7}
STAGE_A = ((0, 8), (0, 6), (1, 6), (1, 7), (0, 3), (1, 3))
STAGE_B = ((0, 7), (0, 5), (1, 5), (0, 2), (1, 2))
STAGE_C = ((0, 4), (1, 4), (0, 1), (1, 1), (0, 0))


def pick(i, values):
    n = len(values)
    total = 0
    for k, value in enumerate(values):
        if value:
            total = total + value * (1 - ((i + n - k) % n + n - 1) // n)
    return total


def remote(src, dst, ssem, rsem, dev):
    return pltpu.make_async_remote_copy(
        src_ref=src, dst_ref=dst, send_sem=ssem, recv_sem=rsem, device_id=dev, device_id_type=MESH
    )


def kernel(
    q_ref, u_ref, pk_ref, pv_ref, rk_ref, rv_ref, behav_ref, cur_ref, adv_ref, len_ref,
    gq_ref, grk_ref, grv_ref, gpk_ref, gpv_ref,
    kv, xkv, qb, ub, gb, gsend, behav, cur, adv, length_s, qt, gt, sc, dp, mx, sm, dl, dqt, dqs,
    part, rs, xself, pp, pc, ps, pz, pt, pr,
    in_s, ag_s, ag_r, rs_s, rs_r, x_s, x_r, pz_s, pz_r, pr_s, pr_r,
    *, nz, nr, tok, heads, prow, full_len,
):
    hd = q_ref.shape[-1]
    scale = hd ** (-0.5)
    rows = tok * heads
    two = 2 * rows
    key_rows = 2 * tok
    per_chunk = key_rows // (2 * prow)
    p_chunks = nz // per_chunk

    c = lax.axis_index("ctx")
    r = lax.axis_index("resp")
    z = c // 2
    h = c % 2
    g = 1 - h
    k = r % 2

    def at_z(off, col):
        return {"ctx": 2 * ((z + off + nz) % nz) + col}

    partner = {"ctx": 2 * z + g}
    other_core = {"resp": r + 1 - 2 * k}

    barrier = pltpu.get_barrier_semaphore()
    near = [partner, other_core]
    for off in (1, 4):
        for sign in (1, -1):
            near += [at_z(sign * off, h), at_z(sign * off, g)]
    near += [at_z(3, h), at_z(-3, h)]
    for dev in near:
        pl.semaphore_signal(barrier, 1, device_id=dev, device_id_type=MESH)

    def from_plane(i):
        return {"resp": (i // 2) * 2 + h, "ctx": 2 * z + i % 2}

    me = (r // 2) * 2 + h
    mine_too = (1 - (k + h) % 2)

    def greet(i, _):
        @pl.when(jnp.logical_or(i != me, k != h))
        def _():
            pl.semaphore_signal(barrier, 1, device_id=from_plane(i), device_id_type=MESH)

        return 0

    lax.fori_loop(0, nr, greet, 0)

    k_at, v_at, pk_at, pv_at = 0, tok, 2 * tok, 2 * tok + prow
    loads = [
        (rk_ref.at[h], kv.at[z, h, pl.ds(k_at, tok)]),
        (rv_ref.at[h], kv.at[z, h, pl.ds(v_at, tok)]),
        (pk_ref, kv.at[z, h, pl.ds(pk_at, prow)]),
        (pv_ref, kv.at[z, h, pl.ds(pv_at, prow)]),
        (rk_ref.at[g], xkv.at[pl.ds(k_at, tok)]),
        (rv_ref.at[g], xkv.at[pl.ds(v_at, tok)]),
        (pk_ref, xkv.at[pl.ds(pk_at, prow)]),
        (pv_ref, xkv.at[pl.ds(pv_at, prow)]),
        (len_ref, length_s),
        (adv_ref, adv),
        (behav_ref, behav),
        (cur_ref, cur),
        (u_ref, ub),
        (q_ref.at[h], qb.at[h]),
    ]
    loads = [pltpu.make_async_copy(src, dst, in_s.at[i]) for i, (src, dst) in enumerate(loads)]
    for load in loads:
        load.start()

    x_kv = remote(xkv, kv.at[z, h], x_s.at[0], x_r.at[0], partner)
    x_kv_in = remote(xkv, kv.at[z, g], x_s.at[0], x_r.at[0], partner)
    x_q = remote(q_ref.at[g], qb.at[h], x_s.at[1], x_r.at[1], partner)
    x_q_in = remote(q_ref.at[g], qb.at[g], x_s.at[1], x_r.at[1], partner)
    x_g = remote(gsend, gb.at[h], x_s.at[2], x_r.at[2], partner)
    x_g_in = remote(gsend, gb.at[g], x_s.at[2], x_r.at[2], partner)

    def down_from(d, o):
        return (z - o + nz) % nz if d == 0 else (z + o) % nz

    def sign(d):
        return 1 - 2 * d

    def ag_own(d, o, col):
        src = kv.at[z, h] if col is h else xkv
        return remote(src, kv.at[z, h], ag_s.at[d, o, col], ag_r.at[d, o, h], at_z(sign(d) * o, col))

    def ag_relay(d, o, hop, blk):
        chunk = down_from(d, o)
        return remote(
            kv.at[chunk, blk], kv.at[chunk, blk], ag_s.at[d, o + hop, blk], ag_r.at[d, o + hop, blk],
            at_z(sign(d) * hop, h),
        )

    def ag_in(d, o, blk):
        chunk = down_from(d, o)
        return remote(kv.at[chunk, blk], kv.at[chunk, blk], ag_s.at[d, o, blk], ag_r.at[d, o, blk], partner)

    for load in loads[:8]:
        load.wait()
    pl.semaphore_wait(barrier, len(near) + nr - mine_too)
    for o in (4, 1):
        for col in (g, h):
            for d in range(2):
                ag_own(d, o, col).start()
    x_kv.start()
    x_q.start()

    for load in loads[8:]:
        load.wait()
    row_of = lax.broadcasted_iota(jnp.int32, (rows, tok), 0) // heads
    col_of = lax.broadcasted_iota(jnp.int32, (rows, tok), 1)
    position = c * tok + lax.broadcasted_iota(jnp.int32, (1, tok), 1)

    def weighted(member):
        length = jnp.full((1, tok), length_s[member], jnp.int32)
        ratio = jnp.minimum(jnp.exp(cur[pl.ds(member, 1), :] - behav[pl.ds(member, 1), :]), RATIO_CAP)
        valid = (position < length).astype(F32)
        weight = -adv[member] * ratio * valid * (full_len / length.astype(F32))
        spread = jnp.where(row_of == col_of, jnp.broadcast_to(weight, (rows, tok)), 0.0)
        column = jnp.sum(spread, axis=1, keepdims=True)
        return (column * ub[member].astype(F32)).astype(BF16)

    gsend[...] = weighted(g)
    x_g.start()
    gb[h] = weighted(h)

    x_kv_in.wait_recv()
    x_q_in.wait_recv()
    qt[...] = qb[...].reshape(two, hd).T
    x_g_in.wait_recv()
    gt[...] = gb[...].reshape(two, hd).T

    def scores_of(keys, values):
        s = jnp.dot(keys, qt[...], preferred_element_type=F32) * scale
        return s, jnp.dot(values, gt[...], preferred_element_type=F32)

    def chunk_of(j, at):
        return kv[j, :, pl.ds(at, tok), :].reshape(key_rows, hd)

    def prompt_of(i, at):
        return kv[pl.ds(i * per_chunk, per_chunk), :, pl.ds(at, prow), :].reshape(key_rows, hd)

    s, grad_p = scores_of(chunk_of(z, k_at), chunk_of(z, v_at))
    key_pos = lax.broadcasted_iota(jnp.int32, (key_rows, two), 0)
    row_pos = lax.broadcasted_iota(jnp.int32, (key_rows, two), 1) // heads
    s = jnp.where(key_pos <= row_pos, s, -jnp.inf)
    sc[z] = s
    dp[z] = grad_p
    m = jnp.max(s, axis=0, keepdims=True)
    e = jnp.exp(s - m)
    mx[...] = m
    sm[...] = jnp.sum(e, axis=0, keepdims=True)
    dl[...] = jnp.sum(e * grad_p, axis=0, keepdims=True)

    def take(j, keys, values):
        s, grad_p = scores_of(keys, values)
        sc[j] = s
        dp[j] = grad_p
        old = mx[...]
        m = jnp.maximum(old, jnp.max(s, axis=0, keepdims=True))
        e = jnp.exp(s - m)
        fix = jnp.exp(old - m)
        mx[...] = m
        sm[...] = sm[...] * fix + jnp.sum(e, axis=0, keepdims=True)
        dl[...] = dl[...] * fix + jnp.sum(e * grad_p, axis=0, keepdims=True)

    def ag_step(i, _):
        o = pick(i, ORDER)
        for blk in (h, g):
            for d in range(2):

                @pl.when(o <= LAST[d])
                def _():
                    ag_in(d, o, blk).wait_recv()

                    @pl.when(jnp.logical_and(o % 3 != 0, o < LAST[d]))
                    def _():
                        ag_relay(d, o, 1, blk).start()

                    @pl.when(o == 4)
                    def _():
                        ag_relay(d, o, 3, blk).start()

        def one(d, _):
            j = (z + (2 * d - 1) * o + nz) % nz

            @pl.when(jnp.logical_and(j < z, o + d < 9))
            def _():
                take(j, chunk_of(j, k_at), chunk_of(j, v_at))

            return 0

        lax.fori_loop(0, 2, one, 0)
        return 0

    lax.fori_loop(0, len(ORDER), ag_step, 0)

    def take_prompt(i, _):
        take(nz + i, prompt_of(i, pk_at), prompt_of(i, pv_at))
        return 0

    lax.fori_loop(0, p_chunks, take_prompt, 0)

    inv = 1.0 / sm[...]
    sm[...] = inv
    dl[...] = dl[...] * inv
    dqt[...] = jnp.zeros_like(dqt)

    def give(j, keys):
        probs = (jnp.exp(sc[j] - mx[...]) * sm[...]).astype(BF16)
        grad_s = (probs.astype(F32) * (dp[j] - dl[...])).astype(BF16)
        d_values = jnp.dot(probs, gb[...].reshape(two, hd), preferred_element_type=F32)
        d_keys = jnp.dot(grad_s, qb[...].reshape(two, hd), preferred_element_type=F32) * scale
        dqt[...] += jnp.dot(keys.T, grad_s, preferred_element_type=F32)
        return d_keys.astype(BF16), d_values.astype(BF16)

    def give_at(d, o):
        j = (z + (2 * d - 1) * o + nz) % nz

        @pl.when(j <= z)
        def _():
            d_keys, d_values = give(j, chunk_of(j, k_at))
            part[d, o, :, pl.ds(k_at, tok), :] = d_keys.reshape(2, tok, hd)
            part[d, o, :, pl.ds(v_at, tok), :] = d_values.reshape(2, tok, hd)

        @pl.when(j > z)
        def _():
            part[d, o] = jnp.zeros((2, 2 * tok, hd), BF16)

    def rs_out(d, o, hop, blk):
        return remote(
            part.at[d, o, blk], rs.at[d, o, blk], rs_s.at[d, o, blk], rs_r.at[d, o, blk],
            {"ctx": 2 * ((z + (2 * d - 1) * hop + nz) % nz) + h},
        )

    def rs_root(d, o, col):
        return remote(
            part.at[d, o, col], rs.at[d, o, h], rs_s.at[d, o, col], rs_r.at[d, o, h], at_z(-sign(d) * o, col)
        )

    def rs_in(d, o, blk):
        return remote(rs.at[d, o, blk], rs.at[d, o, blk], rs_s.at[d, o, blk], rs_r.at[d, o, blk], partner)

    def stage_a(i, _):
        d = pick(i, [d for d, _ in STAGE_A])
        o = pick(i, [o for _, o in STAGE_A])
        hop = pick(i, [o - PARENT[o] for _, o in STAGE_A])
        give_at(d, o)
        for blk in range(2):
            rs_out(d, o, hop, blk).start()
        return 0

    lax.fori_loop(0, len(STAGE_A), stage_a, 0)

    def give_prompt(i, _):
        d_keys, d_values = give(nz + i, prompt_of(i, pk_at))
        d_keys = d_keys.reshape(per_chunk, 2, prow, hd)
        d_values = d_values.reshape(per_chunk, 2, prow, hd)
        for blk in range(2):
            pp[blk, pl.ds(i * per_chunk, per_chunk), pl.ds(0, prow), :] = d_keys[:, blk]
            pp[blk, pl.ds(i * per_chunk, per_chunk), pl.ds(prow, prow), :] = d_values[:, blk]
        return 0

    lax.fori_loop(0, p_chunks, give_prompt, 0)
    x_core = remote(pp.at[1 - k], pc, x_s.at[4], x_r.at[4], other_core)
    x_core.start()

    def stage_b(i, _):
        give_at(pick(i, [d for d, _ in STAGE_B]), pick(i, [o for _, o in STAGE_B]))
        return 0

    lax.fori_loop(0, len(STAGE_B), stage_b, 0)

    x_core.wait_recv()
    ps[...] = (pp[k].astype(F32) + pc[...].astype(F32)).astype(BF16)

    def pz_out(i):
        to = (z + i) % nz
        return remote(ps.at[to], pz.at[z], pz_s.at[i], pz_r.at[z], {"ctx": 2 * to + h})

    def pz_in(i):
        src = (z + i) % nz
        return remote(ps.at[src], pz.at[src], pz_s.at[i], pz_r.at[src], {"ctx": 2 * src + h})

    def send_pz(i, _):
        pz_out(i).start()
        return 0

    lax.fori_loop(1, nz, send_pz, 0)

    def join(d, o, children):
        for blk in range(2):
            for child in children:
                rs_in(d, child, blk).wait_recv()
            total = part[d, o, blk].astype(F32)
            for child in children:
                total = total + rs[d, child, blk].astype(F32)
            part[d, o, blk] = total.astype(BF16)
            if PARENT[o]:
                rs_out(d, o, o - PARENT[o], blk).start()
            else:
                rs_root(d, o, blk).start()

    for d, o in STAGE_B:
        join(d, o, [child for child in PARENT if PARENT[child] == o and child <= LAST[d]])

    def stage_c(i, _):
        give_at(pick(i, [d for d, _ in STAGE_C]), pick(i, [o for _, o in STAGE_C]))
        return 0

    lax.fori_loop(0, len(STAGE_C), stage_c, 0)

    x_own = remote(part.at[0, 0, g], xself, x_s.at[5], x_r.at[5], partner)
    x_own.start()

    for d, o in STAGE_C[:-1]:
        join(d, o, [child for child in PARENT if PARENT[child] == o and child <= LAST[d]])

    dqs[...] = (dqt[...] * scale).T.astype(BF16).reshape(2, rows, hd)
    x_dq = remote(dqs.at[g], gq_ref.at[h], x_s.at[3], x_r.at[3], partner)
    x_dq_in = remote(dqs.at[g], gq_ref.at[g], x_s.at[3], x_r.at[3], partner)
    x_dq.start()
    gq_ref[h] = dqs[h]

    def wait_pz(i, total):
        pz_in(i).wait_recv()
        return total + pz[(z + i) % nz].astype(F32)

    pt[...] = lax.fori_loop(1, nz, wait_pz, ps[z].astype(F32))

    def pr_out(i):
        return remote(pt, pr.at[me], pr_s.at[i], pr_r.at[me], {"resp": (r + i) % nr, "ctx": 2 * z + k})

    def pr_in(i):
        return remote(pt, pr.at[i], pr_s.at[i], pr_r.at[i], partner)

    @pl.when(k == h)
    def _():
        pr[me] = pt[...]

    def send_pr(i, _):
        @pl.when(jnp.logical_or(i != 0, k != h))
        def _():
            pr_out(i).start()

        return 0

    lax.fori_loop(0, nr, send_pr, 0)

    def total_of(own, member):
        total = own.astype(F32)
        for d, o in STAGE_C[:-1]:
            total = total + rs[d, o, member].astype(F32)
        return total.astype(BF16)

    x_own.wait_recv()
    for member in range(2):
        for d, o in STAGE_C[:-1]:
            rs_in(d, o, member).wait_recv()
    mine = total_of(part[0, 0, h], h)
    grk_ref[h] = mine[:tok]
    grv_ref[h] = mine[tok:]
    theirs = total_of(xself[...], g)
    grk_ref[g] = theirs[:tok]
    grv_ref[g] = theirs[tok:]

    def wait_pr(i, _):
        @pl.when(jnp.logical_or(i != me, k != h))
        def _():
            pr_in(i).wait_recv()

        return 0

    lax.fori_loop(0, nr, wait_pr, 0)
    total = pr[0]
    for i in range(1, nr):
        total = total + pr[i]
    gpk_ref[...] = total[:prow]
    gpv_ref[...] = total[prow:]
    x_dq_in.wait_recv()

    for item in (x_kv, x_q, x_g, x_dq, x_core, x_own):
        item.wait_send()
    for d in range(2):
        for o in range(1, LAST[d] + 1):
            for blk in range(2):
                ag_in(d, o, blk).wait_send()
                rs_in(d, o, blk).wait_send()

    def sent(i, _):
        @pl.when(i != 0)
        def _():
            pz_out(i).wait_send()

        @pl.when(jnp.logical_or(i != 0, k != h))
        def _():
            pr_out(i).wait_send()

        return 0

    lax.fori_loop(0, nr, sent, 0)


def write_out(*refs):
    n = len(refs) // 2
    sems = refs[-1]
    copies = [pltpu.make_async_copy(refs[i], refs[n + i], sems.at[i]) for i in range(n)]
    for copy in copies:
        copy.start()
    for copy in copies:
        copy.wait()


def per_device(queries, prompt_keys, prompt_values, resp_keys, resp_values, upstream, behav_logp, cur_logp, advantages, lengths):
    members, tok, heads, hd = queries.shape
    nc = lax.axis_size("ctx")
    nr = lax.axis_size("resp")
    nz = nc // 2
    prow = prompt_keys.shape[0]
    rows = tok * heads
    two = 2 * rows
    key_rows = 2 * tok
    blk = 2 * tok + 2 * prow
    slots = nz + (nc * prow) // key_rows
    vmem = pl.BlockSpec(memory_space=pltpu.VMEM)
    hbm = pl.BlockSpec(memory_space=pltpu.HBM)
    dma = pltpu.SemaphoreType.DMA
    offs = max(LAST) + 1
    shapes = (
        jax.ShapeDtypeStruct((members, rows, hd), BF16),
        jax.ShapeDtypeStruct((members, tok, hd), BF16),
        jax.ShapeDtypeStruct((members, tok, hd), BF16),
        jax.ShapeDtypeStruct((prow, hd), F32),
        jax.ShapeDtypeStruct((prow, hd), F32),
    )
    outs = pl.pallas_call(
        functools.partial(kernel, nz=nz, nr=nr, tok=tok, heads=heads, prow=prow, full_len=tok * nc),
        name="grpo_backward",
        out_shape=shapes,
        in_specs=[hbm] * 10,
        out_specs=(vmem,) * 5,
        scratch_shapes=[
            pltpu.VMEM((nz, 2, blk, hd), BF16),
            pltpu.VMEM((blk, hd), BF16),
            pltpu.VMEM((2, rows, hd), BF16),
            pltpu.VMEM((2, rows, hd), BF16),
            pltpu.VMEM((2, rows, hd), BF16),
            pltpu.VMEM((rows, hd), BF16),
            pltpu.VMEM((members, tok), F32),
            pltpu.VMEM((members, tok), F32),
            pltpu.SMEM((members,), F32),
            pltpu.SMEM((members,), jnp.int32),
            pltpu.VMEM((hd, two), BF16),
            pltpu.VMEM((hd, two), BF16),
            pltpu.VMEM((slots, key_rows, two), F32),
            pltpu.VMEM((slots, key_rows, two), F32),
            pltpu.VMEM((1, two), F32),
            pltpu.VMEM((1, two), F32),
            pltpu.VMEM((1, two), F32),
            pltpu.VMEM((hd, two), F32),
            pltpu.VMEM((2, rows, hd), BF16),
            pltpu.VMEM((2, offs, 2, 2 * tok, hd), BF16),
            pltpu.VMEM((2, offs, 2, 2 * tok, hd), BF16),
            pltpu.VMEM((2 * tok, hd), BF16),
            pltpu.VMEM((2, nz, 2 * prow, hd), BF16),
            pltpu.VMEM((nz, 2 * prow, hd), BF16),
            pltpu.VMEM((nz, 2 * prow, hd), BF16),
            pltpu.VMEM((nz, 2 * prow, hd), BF16),
            pltpu.VMEM((2 * prow, hd), F32),
            pltpu.VMEM((nr, 2 * prow, hd), F32),
            dma((14,)),
            dma((2, offs, 2)),
            dma((2, offs, 2)),
            dma((2, offs, 2)),
            dma((2, offs, 2)),
            dma((6,)),
            dma((6,)),
            dma((nz,)),
            dma((nz,)),
            dma((nr,)),
            dma((nr,)),
        ],
        compiler_params=pltpu.CompilerParams(
            collective_id=0, has_side_effects=True, vmem_limit_bytes=48 * 1024 * 1024
        ),
    )(
        queries.reshape(members, rows, hd),
        upstream.reshape(members, rows, hd),
        prompt_keys, prompt_values, resp_keys, resp_values, behav_logp, cur_logp, advantages, lengths,
    )
    outs = (outs[0].reshape(queries.shape), *outs[1:])
    return pl.pallas_call(
        write_out,
        name="write_out",
        out_shape=tuple(jax.ShapeDtypeStruct(o.shape, o.dtype) for o in outs),
        in_specs=[vmem] * 5,
        out_specs=(hbm,) * 5,
        scratch_shapes=[dma((5,))],
    )(*outs)


def solution(mesh):
    placed = (
        P("resp", "ctx", None, None),
        P("ctx", None),
        P("ctx", None),
        P("resp", "ctx", None),
        P("resp", "ctx", None),
        P("resp", "ctx", None, None),
        P("resp", "ctx"),
        P("resp", "ctx"),
        P("resp"),
        P("resp"),
    )
    return jax.shard_map(
        per_device,
        mesh=mesh,
        in_specs=placed,
        out_specs=(
            P("resp", "ctx", None, None),
            P("resp", "ctx", None),
            P("resp", "ctx", None),
            P("ctx", None),
            P("ctx", None),
        ),
        check_vma=False,
    )
```

```python
import functools

import jax
import jax.numpy as jnp
from jax import lax
from jax.experimental import pallas as pl
from jax.experimental.pallas import tpu as pltpu
from jax.sharding import PartitionSpec as P

RATIO_CAP = 2.0
VMEM_BYTES = 63 * 1024 * 1024
MESH = pl.DeviceIdType.MESH
F32 = jnp.float32
BF16 = jnp.bfloat16
LAST = (8, 7)
ORDER = (1, 4, 2, 5, 7, 3, 6, 8)
PARENT = {1: 0, 2: 1, 3: 2, 4: 0, 5: 4, 6: 5, 7: 4, 8: 7}
STAGE_A = ((0, 8), (0, 6), (1, 6), (1, 7), (0, 3), (1, 3))
STAGE_B = ((0, 7), (0, 5), (1, 5), (0, 2), (1, 2))
STAGE_C = ((0, 4), (1, 4), (0, 1), (1, 1), (0, 0))
ROOTS = ((0, 4), (1, 4), (0, 1), (1, 1))
FIRST = (4, 3, 1)
THEN = {4: (8, 7, 5), 3: (6,), 1: (2,)}


def pick(i, values):
    n = len(values)
    total = i * 0
    for k, value in enumerate(values):
        if value:
            total = total + value * (1 - ((i + n - k) % n + n - 1) // n)
    return total


def reach(o):
    return max([o] + [reach(child) for child in PARENT if PARENT[child] == o and child <= LAST[1]])


def children(d, o):
    return [child for child in PARENT if PARENT[child] == o and child <= LAST[d]]


def remote(src, dst, ssem, rsem, dev):
    return pltpu.make_async_remote_copy(
        src_ref=src, dst_ref=dst, send_sem=ssem, recv_sem=rsem, device_id=dev, device_id_type=MESH
    )


def kernel(
    q_ref, u_ref, pk_ref, pv_ref, rk_ref, rv_ref, behav_ref, cur_ref, adv_ref, len_ref,
    gq_ref, grk_ref, grv_ref, gpk_ref, gpv_ref,
    kv, xkv, own_p, pkv, qb, ub, gb, gsend, behav, cur, adv, length_s, qt, gt, sc, dp, mx, sm, dl, dqt, dqs,
    part, rs, xself, pp, pc, pt, pz, pf,
    in_s, ag_s, ag_r, rs_s, rs_r, x_s, x_r, pm_s, pm_r, pl_s, pl_r, pa_s, pa_r, pz_s, pz_r, pf_s, pf_r,
    *, nz, nr, tok, heads, prow, full_len,
):
    hd = q_ref.shape[-1]
    scale = hd ** (-0.5)
    rows = tok * heads
    two = 2 * rows
    key_rows = 2 * tok
    shards = 2 * nr
    per_chunk = key_rows // prow
    p_chunks = shards // per_chunk

    r = lax.axis_index("resp")
    c = lax.axis_index("ctx")
    z = c // 2
    h = c % 2
    g = 1 - h
    p = 2 * r + h

    def at_z(off, col):
        return {"ctx": 2 * ((z + off + nz) % nz) + col}

    def in_plane(i):
        q = (p + i) % shards
        return q, {"resp": q // 2, "ctx": 2 * z + q % 2}

    partner = {"ctx": 2 * z + g}

    loads = [
        (rk_ref.at[g], xkv.at[pl.ds(0, tok)]),
        (rv_ref.at[g], xkv.at[pl.ds(tok, tok)]),
        (rk_ref.at[h], kv.at[z, h, pl.ds(0, tok)]),
        (rv_ref.at[h], kv.at[z, h, pl.ds(tok, tok)]),
        (pk_ref, own_p.at[pl.ds(0, prow)]),
        (pv_ref, own_p.at[pl.ds(prow, prow)]),
        (len_ref, length_s),
        (adv_ref, adv),
        (behav_ref, behav),
        (cur_ref, cur),
        (u_ref, ub),
        (q_ref.at[h], qb.at[h]),
    ]
    loads = [pltpu.make_async_copy(src, dst, in_s.at[i]) for i, (src, dst) in enumerate(loads)]
    for load in loads:
        load.start()

    barrier = pltpu.get_barrier_semaphore()
    for hop in (4, 3, 1):
        for way in (1, -1):
            pl.semaphore_signal(barrier, 1, device_id=at_z(way * hop, h), device_id_type=MESH)

    def greet(i, _):
        pl.semaphore_signal(barrier, 1, device_id=in_plane(i)[1], device_id_type=MESH)
        return 0

    lax.fori_loop(1, shards, greet, 0)
    x_kv = remote(xkv, kv.at[z, h], x_s.at[0], x_r.at[0], partner)
    x_kv_in = remote(xkv, kv.at[z, g], x_s.at[0], x_r.at[0], partner)
    x_q = remote(q_ref.at[g], qb.at[h], x_s.at[1], x_r.at[1], partner)
    x_q_in = remote(q_ref.at[g], qb.at[g], x_s.at[1], x_r.at[1], partner)
    x_g = remote(gsend, gb.at[h], x_s.at[2], x_r.at[2], partner)
    x_g_in = remote(gsend, gb.at[g], x_s.at[2], x_r.at[2], partner)

    def chunk_at(d, o):
        return (z + (2 * d - 1) * o + nz) % nz

    def edge_in(d, o, far):
        return z >= o if d == 0 else chunk_at(1, o) < far

    def edge_out(d, o, child, far):
        if d == 0:
            return jnp.logical_and(z >= o, z + child - o < nz)
        return chunk_at(1, o) < far

    def ag_out(d, o, child, blk):
        chunk = chunk_at(d, o)
        return remote(
            kv.at[chunk, blk], kv.at[chunk, blk], ag_s.at[d, child, blk], ag_r.at[d, child, blk],
            at_z((1 - 2 * d) * (child - o), h),
        )

    def ag_in(d, o, blk):
        chunk = chunk_at(d, o)
        return remote(kv.at[chunk, blk], kv.at[chunk, blk], ag_s.at[d, o, blk], ag_r.at[d, o, blk], partner)

    def ag_send(d, o, child, far, blk):
        @pl.when(edge_out(d, o, child, far))
        def _():
            ag_out(d, o, child, blk).start()

    ahead = (z - r + nz) % nz

    def pm_out(d, o, child):
        return remote(pkv.at[p], pkv.at[p], pm_s.at[d, child], pm_r.at[0], at_z((1 - 2 * d) * (child - o), h))

    def pm_at(d, o):
        return ahead == (o if d == 0 else nz - o)

    def pl_out(i):
        return remote(pkv.at[p], pkv.at[p], pl_s.at[i], pl_r.at[p], in_plane(i)[1])

    def pl_in(i):
        q, dev = in_plane(i)
        return remote(pkv.at[q], pkv.at[q], pl_s.at[i], pl_r.at[q], dev)

    def send_plane():
        def one(i, _):
            pl_out(i).start()
            return 0

        lax.fori_loop(1, shards, one, 0)

    for load in loads[:6]:
        load.wait()
    pl.semaphore_wait(barrier, 6 + shards - 1)
    x_kv.start()
    for d, o in ROOTS:
        ag_send(d, 0, o, reach(o), h)
    x_q.start()

    @pl.when(z == r)
    def _():
        pkv[p] = own_p[...]
        for o in FIRST:
            for d in range(2):
                pm_out(d, 0, o).start()

    row_of = lax.broadcasted_iota(jnp.int32, (rows, tok), 0) // heads
    col_of = lax.broadcasted_iota(jnp.int32, (rows, tok), 1)

    position = c * tok + lax.broadcasted_iota(jnp.int32, (1, tok), 1)
    for load in loads[6:]:
        load.wait()

    def weighted(member):
        length = jnp.full((1, tok), length_s[member], jnp.int32)
        ratio = jnp.minimum(jnp.exp(cur[pl.ds(member, 1), :] - behav[pl.ds(member, 1), :]), RATIO_CAP)
        valid = (position < length).astype(F32)
        weight = -adv[member] * ratio * valid * (full_len / length.astype(F32))
        spread = jnp.where(row_of == col_of, jnp.broadcast_to(weight, (rows, tok)), 0.0)
        column = jnp.sum(spread, axis=1, keepdims=True)
        return (column * ub[member].astype(F32)).astype(BF16)

    gsend[...] = weighted(g)
    x_g.start()

    @pl.when(z == r)
    def _():
        send_plane()

    gb[h] = weighted(h)
    x_kv_in.wait_recv()
    for d, o in ROOTS:
        ag_send(d, 0, o, reach(o), g)

    def ag_step(i):
        o = pick(i, ORDER)
        far = pick(i, [reach(o) if o <= LAST[1] else 0 for o in ORDER])
        far_next = pick(i, [reach(o + 1) if o + 1 in children(1, o) else 0 for o in ORDER])
        for blk in (h, g):
            for d in range(2):

                @pl.when(edge_in(d, o, far))
                def _():
                    ag_in(d, o, blk).wait_recv()

                    @pl.when(o == 4)
                    def _():
                        ag_send(d, 4, 7, reach(7), blk)

                    @pl.when(jnp.logical_and(o % 3 != 0, o < LAST[d]))
                    def _():
                        ag_send(d, o, o + 1, far_next, blk)

    def is_first():
        at = [pm_at(d, o) for d in range(2) for o in FIRST]
        return functools.reduce(jnp.logical_or, at)

    def pm_first():
        @pl.when(is_first())
        def _():
            pm_out(0, 0, 1).wait_recv()
            for d in range(2):
                for o in FIRST:

                    @pl.when(pm_at(d, o))
                    def _():
                        for child in THEN[o]:
                            if child <= LAST[d]:
                                pm_out(d, o, child).start()

            send_plane()

    def pm_then():
        @pl.when(jnp.logical_not(jnp.logical_or(is_first(), ahead == 0)))
        def _():
            pm_out(0, 0, 1).wait_recv()
            send_plane()

    def scores_of(keys, values):
        s = jnp.dot(keys, qt[...], preferred_element_type=F32) * scale
        return s, jnp.dot(values, gt[...], preferred_element_type=F32)

    def chunk_of(j, at):
        return kv[j, :, pl.ds(at, tok), :].reshape(key_rows, hd)

    def prompt_of(i, at):
        return pkv[pl.ds(i * per_chunk, per_chunk), pl.ds(at, prow), :].reshape(key_rows, hd)

    def take(j, keys, values):
        s, grad_p = scores_of(keys, values)
        sc[j] = s
        dp[j] = grad_p
        old = mx[...]
        m = jnp.maximum(old, jnp.max(s, axis=0, keepdims=True))
        e = jnp.exp(s - m)
        fix = jnp.exp(old - m)
        mx[...] = m
        sm[...] = sm[...] * fix + jnp.sum(e, axis=0, keepdims=True)
        dl[...] = dl[...] * fix + jnp.sum(e * grad_p, axis=0, keepdims=True)

    def take_pair(i):
        o = pick(i, ORDER)

        def one(d, _):
            j = chunk_at(d, o)

            @pl.when(jnp.logical_and(j < z, o + d < 9))
            def _():
                take(j, chunk_of(j, 0), chunk_of(j, tok))

            return 0

        lax.fori_loop(0, 2, one, 0)

    def early(i, _):
        ag_step(i)
        return 0

    ag_step(jnp.int32(0))
    pm_first()
    lax.fori_loop(1, 3, early, 0)
    pm_then()

    x_q_in.wait_recv()
    qt[...] = qb[...].reshape(two, hd).T
    x_g_in.wait_recv()
    gt[...] = gb[...].reshape(two, hd).T
    s, grad_p = scores_of(chunk_of(z, 0), chunk_of(z, tok))
    key_pos = lax.broadcasted_iota(jnp.int32, (key_rows, two), 0)
    row_pos = lax.broadcasted_iota(jnp.int32, (key_rows, two), 1) // heads
    s = jnp.where(key_pos <= row_pos, s, -jnp.inf)
    sc[z] = s
    dp[z] = grad_p
    m = jnp.max(s, axis=0, keepdims=True)
    e = jnp.exp(s - m)
    mx[...] = m
    sm[...] = jnp.sum(e, axis=0, keepdims=True)
    dl[...] = jnp.sum(e * grad_p, axis=0, keepdims=True)

    def behind(i, _):
        @pl.when(i > 2)
        def _():
            ag_step(i)

        take_pair(i)
        return 0

    lax.fori_loop(0, len(ORDER), behind, 0)

    def wait_plane(i, _):
        pl_in(i).wait_recv()
        return 0

    lax.fori_loop(1, shards, wait_plane, 0)

    def take_prompt(i, _):
        take(nz + i, prompt_of(i, 0), prompt_of(i, prow))
        return 0

    lax.fori_loop(0, p_chunks, take_prompt, 0)

    inv = 1.0 / sm[...]
    sm[...] = inv
    dl[...] = dl[...] * inv
    dqt[...] = jnp.zeros_like(dqt)

    def give(j, keys):
        probs = (jnp.exp(sc[j] - mx[...]) * sm[...]).astype(BF16)
        grad_s = (probs.astype(F32) * (dp[j] - dl[...])).astype(BF16)
        d_values = jnp.dot(probs, gb[...].reshape(two, hd), preferred_element_type=F32)
        d_keys = jnp.dot(grad_s, qb[...].reshape(two, hd), preferred_element_type=F32) * scale
        dqt[...] += jnp.dot(keys.T, grad_s, preferred_element_type=F32)
        return d_keys.astype(BF16), d_values.astype(BF16)

    def pa_out(i):
        q, dev = in_plane(i)
        return remote(pp.at[q], pc.at[p], pa_s.at[i], pa_r.at[p], dev)

    def pa_in(i):
        q, dev = in_plane(i)
        return remote(pp.at[q], pc.at[q], pa_s.at[i], pa_r.at[q], dev)

    def give_prompt(i, _):
        d_keys, d_values = give(nz + i, prompt_of(i, 0))
        pp[pl.ds(i * per_chunk, per_chunk), pl.ds(0, prow), :] = d_keys.reshape(per_chunk, prow, hd)
        pp[pl.ds(i * per_chunk, per_chunk), pl.ds(prow, prow), :] = d_values.reshape(per_chunk, prow, hd)
        return 0

    lax.fori_loop(0, p_chunks, give_prompt, 0)

    def send_pa(i, _):
        pa_out(i).start()
        return 0

    lax.fori_loop(1, shards, send_pa, 0)

    def give_at(d, o):
        j = chunk_at(d, o)

        @pl.when(j <= z)
        def _():
            d_keys, d_values = give(j, chunk_of(j, 0))
            part[d, o, :, pl.ds(0, tok), :] = d_keys.reshape(2, tok, hd)
            part[d, o, :, pl.ds(tok, tok), :] = d_values.reshape(2, tok, hd)

        @pl.when(j > z)
        def _():
            part[d, o] = jnp.zeros((2, 2 * tok, hd), BF16)

    def rs_out(d, o, hop, blk):
        return remote(
            part.at[d, o, blk], rs.at[d, o, blk], rs_s.at[d, o, blk], rs_r.at[d, o, blk], at_z((2 * d - 1) * hop, h)
        )

    def rs_root(d, o, col):
        return remote(
            part.at[d, o, col], rs.at[d, o, h], rs_s.at[d, o, col], rs_r.at[d, o, h], at_z((2 * d - 1) * o, col)
        )

    def rs_in(d, o, blk):
        return remote(rs.at[d, o, blk], rs.at[d, o, blk], rs_s.at[d, o, blk], rs_r.at[d, o, blk], partner)

    def stage_a(i, _):
        d = pick(i, [d for d, _ in STAGE_A])
        o = pick(i, [o for _, o in STAGE_A])
        hop = pick(i, [o - PARENT[o] for _, o in STAGE_A])
        far = pick(i, [reach(o) if d else 0 for d, o in STAGE_A])
        give_at(d, o)

        @pl.when(jnp.logical_or(jnp.logical_and(d == 0, z >= o), jnp.logical_and(d == 1, chunk_at(1, o) < far)))
        def _():
            for blk in range(2):
                rs_out(d, o, hop, blk).start()

        return 0

    lax.fori_loop(0, len(STAGE_A), stage_a, 0)

    def stage_b(i, _):
        give_at(pick(i, [d for d, _ in STAGE_B]), pick(i, [o for _, o in STAGE_B]))
        return 0

    lax.fori_loop(0, len(STAGE_B), stage_b, 0)

    def join(d, o):
        @pl.when(edge_in(d, o, reach(o)))
        def _():
            for blk in range(2):
                for child in children(d, o):

                    @pl.when(edge_out(d, o, child, reach(child)))
                    def _():
                        rs_in(d, child, blk).wait_recv()
                        part[d, o, blk] = (part[d, o, blk].astype(F32) + rs[d, child, blk].astype(F32)).astype(BF16)

                if PARENT[o]:
                    rs_out(d, o, o - PARENT[o], blk).start()
                else:
                    rs_root(d, o, blk).start()

    for d, o in STAGE_B:
        join(d, o)

    def wait_pa(i, total):
        pa_in(i).wait_recv()
        return total + pc[(p + i) % shards].astype(F32)

    pt[...] = lax.fori_loop(1, shards, wait_pa, pp[p].astype(F32))
    pz_out = remote(pt, pz.at[z], pz_s.at[0], pz_r.at[z], at_z(r - z, h))

    @pl.when(z != r)
    def _():
        pz_out.start()

    def stage_c(i, _):
        give_at(pick(i, [d for d, _ in STAGE_C]), pick(i, [o for _, o in STAGE_C]))
        return 0

    lax.fori_loop(0, len(STAGE_C), stage_c, 0)

    x_own = remote(part.at[0, 0, g], xself, x_s.at[4], x_r.at[4], partner)
    x_own.start()

    for d, o in ROOTS:
        join(d, o)

    dqs[...] = (dqt[...] * scale).T.astype(BF16).reshape(2, rows, hd)
    x_dq = remote(dqs.at[g], gq_ref.at[h], x_s.at[3], x_r.at[3], partner)
    x_dq_in = remote(dqs.at[g], gq_ref.at[g], x_s.at[3], x_r.at[3], partner)
    x_dq.start()
    gq_ref[h] = dqs[h]

    def pf_out(i):
        return remote(pf, pf, pf_s.at[i], pf_r.at[0], {"resp": (r + i) % nr})

    @pl.when(z == r)
    def _():
        def wait_pz(i, total):
            src = (z + i) % nz
            remote(pt, pz.at[src], pz_s.at[0], pz_r.at[src], partner).wait_recv()
            return total + pz[src]

        pf[...] = lax.fori_loop(1, nz, wait_pz, pt[...])

        def send_pf(i, _):
            pf_out(i).start()
            return 0

        lax.fori_loop(1, nr, send_pf, 0)

    def total_of(own, member):
        total = own.astype(F32)
        for d, o in ROOTS:
            total = total + rs[d, o, member].astype(F32)
        return total.astype(BF16)

    for member in range(2):
        for d, o in ROOTS:
            used = edge_out(d, 0, o, reach(o))

            @pl.when(used)
            def _():
                rs_in(d, o, member).wait_recv()

            @pl.when(jnp.logical_not(used))
            def _():
                rs[d, o, member] = jnp.zeros((2 * tok, hd), BF16)

    mine = total_of(part[0, 0, h], h)
    grk_ref[h] = mine[:tok]
    grv_ref[h] = mine[tok:]
    x_own.wait_recv()
    theirs = total_of(xself[...], g)
    grk_ref[g] = theirs[:tok]
    grv_ref[g] = theirs[tok:]

    for item in (x_kv, x_q, x_g, x_dq, x_own):
        item.wait_send()
    for d in range(2):
        for o in range(1, LAST[d] + 1):

            @pl.when(edge_out(d, PARENT[o], o, reach(o) if d else 0))
            def _():
                for blk in range(2):
                    ag_in(d, o, blk).wait_send()

            @pl.when(edge_in(d, o, reach(o) if d else 0))
            def _():
                for blk in range(2):
                    rs_in(d, o, blk).wait_send()


    for d in range(2):
        for o in FIRST:

            @pl.when(ahead == 0)
            def _():
                pm_out(d, 0, o).wait_send()

            @pl.when(pm_at(d, o))
            def _():
                for child in THEN[o]:
                    if child <= LAST[d]:
                        pm_out(d, o, child).wait_send()

    def sent(i, _):
        pl_out(i).wait_send()
        pa_out(i).wait_send()
        return 0

    lax.fori_loop(1, shards, sent, 0)

    x_dq_in.wait_recv()

    @pl.when(z != r)
    def _():
        pz_out.wait_send()
        pf_out(0).wait_recv()

    @pl.when(z == r)
    def _():
        def sent_pf(i, _):
            pf_out(i).wait_send()
            return 0

        lax.fori_loop(1, nr, sent_pf, 0)

    gpk_ref[...] = pf[:prow]
    gpv_ref[...] = pf[prow:]


def write_out(*refs):
    n = len(refs) // 2
    sems = refs[-1]
    copies = [pltpu.make_async_copy(refs[i], refs[n + i], sems.at[i]) for i in range(n)]
    for copy in copies:
        copy.start()
    for copy in copies:
        copy.wait()


def per_device(queries, prompt_keys, prompt_values, resp_keys, resp_values, upstream, behav_logp, cur_logp, advantages, lengths):
    members, tok, heads, hd = queries.shape
    nc = lax.axis_size("ctx")
    nr = lax.axis_size("resp")
    nz = nc // 2
    prow = prompt_keys.shape[0]
    rows = tok * heads
    two = 2 * rows
    key_rows = 2 * tok
    shards = 2 * nr
    slots = nz + (nc * prow) // key_rows
    vmem = pl.BlockSpec(memory_space=pltpu.VMEM)
    hbm = pl.BlockSpec(memory_space=pltpu.HBM)
    dma = pltpu.SemaphoreType.DMA
    offs = max(LAST) + 1
    shapes = (
        jax.ShapeDtypeStruct((members, rows, hd), BF16),
        jax.ShapeDtypeStruct((members, tok, hd), BF16),
        jax.ShapeDtypeStruct((members, tok, hd), BF16),
        jax.ShapeDtypeStruct((prow, hd), F32),
        jax.ShapeDtypeStruct((prow, hd), F32),
    )
    outs = pl.pallas_call(
        functools.partial(kernel, nz=nz, nr=nr, tok=tok, heads=heads, prow=prow, full_len=tok * nc),
        name="grpo_backward",
        out_shape=shapes,
        in_specs=[hbm] * 10,
        out_specs=(vmem,) * 5,
        scratch_shapes=[
            pltpu.VMEM((nz, 2, 2 * tok, hd), BF16),
            pltpu.VMEM((2 * tok, hd), BF16),
            pltpu.VMEM((2 * prow, hd), BF16),
            pltpu.VMEM((shards, 2 * prow, hd), BF16),
            pltpu.VMEM((2, rows, hd), BF16),
            pltpu.VMEM((2, rows, hd), BF16),
            pltpu.VMEM((2, rows, hd), BF16),
            pltpu.VMEM((rows, hd), BF16),
            pltpu.VMEM((members, tok), F32),
            pltpu.VMEM((members, tok), F32),
            pltpu.SMEM((members,), F32),
            pltpu.SMEM((members,), jnp.int32),
            pltpu.VMEM((hd, two), BF16),
            pltpu.VMEM((hd, two), BF16),
            pltpu.VMEM((slots, key_rows, two), F32),
            pltpu.VMEM((slots, key_rows, two), F32),
            pltpu.VMEM((1, two), F32),
            pltpu.VMEM((1, two), F32),
            pltpu.VMEM((1, two), F32),
            pltpu.VMEM((hd, two), F32),
            pltpu.VMEM((2, rows, hd), BF16),
            pltpu.VMEM((2, offs, 2, 2 * tok, hd), BF16),
            pltpu.VMEM((2, offs, 2, 2 * tok, hd), BF16),
            pltpu.VMEM((2 * tok, hd), BF16),
            pltpu.VMEM((shards, 2 * prow, hd), BF16),
            pltpu.VMEM((shards, 2 * prow, hd), BF16),
            pltpu.VMEM((2 * prow, hd), F32),
            pltpu.VMEM((nz, 2 * prow, hd), F32),
            pltpu.VMEM((2 * prow, hd), F32),
            dma((12,)),
            dma((2, offs, 2)),
            dma((2, offs, 2)),
            dma((2, offs, 2)),
            dma((2, offs, 2)),
            dma((5,)),
            dma((5,)),
            dma((2, offs)),
            dma((1,)),
            dma((shards,)),
            dma((shards,)),
            dma((shards,)),
            dma((shards,)),
            dma((1,)),
            dma((nz,)),
            dma((nr,)),
            dma((1,)),
        ],
        compiler_params=pltpu.CompilerParams(
            collective_id=0, has_side_effects=True, vmem_limit_bytes=VMEM_BYTES
        ),
    )(
        queries.reshape(members, rows, hd),
        upstream.reshape(members, rows, hd),
        prompt_keys, prompt_values, resp_keys, resp_values, behav_logp, cur_logp, advantages, lengths,
    )
    outs = (outs[0].reshape(queries.shape), *outs[1:])
    return pl.pallas_call(
        write_out,
        name="write_out",
        out_shape=tuple(jax.ShapeDtypeStruct(o.shape, o.dtype) for o in outs),
        in_specs=[vmem] * 5,
        out_specs=(hbm,) * 5,
        scratch_shapes=[dma((5,))],
        compiler_params=pltpu.CompilerParams(vmem_limit_bytes=VMEM_BYTES),
    )(*outs)


def solution(mesh):
    placed = (
        P("resp", "ctx", None, None),
        P("ctx", None),
        P("ctx", None),
        P("resp", "ctx", None),
        P("resp", "ctx", None),
        P("resp", "ctx", None, None),
        P("resp", "ctx"),
        P("resp", "ctx"),
        P("resp"),
        P("resp"),
    )
    return jax.shard_map(
        per_device,
        mesh=mesh,
        in_specs=placed,
        out_specs=(
            P("resp", "ctx", None, None),
            P("resp", "ctx", None),
            P("resp", "ctx", None),
            P("ctx", None),
            P("ctx", None),
        ),
        check_vma=False,
    )
```

```python
import functools

import jax
import jax.numpy as jnp
from jax import lax
from jax.experimental import pallas as pl
from jax.experimental.pallas import tpu as pltpu
from jax.sharding import PartitionSpec as P

RATIO_CAP = 2.0
VMEM_BYTES = 63 * 1024 * 1024
MESH = pl.DeviceIdType.MESH
F32 = jnp.float32
BF16 = jnp.bfloat16
LAST = (8, 7)
ORDER = (1, 4, 2, 5, 7, 3, 6, 8)
PARENT = {1: 0, 2: 1, 3: 2, 4: 0, 5: 4, 6: 5, 7: 4, 8: 7}
STAGE_A = ((0, 8), (0, 6), (1, 6), (1, 7), (0, 3), (1, 3))
STAGE_B = ((0, 7), (0, 5), (1, 5), (0, 2), (1, 2))
STAGE_C = ((0, 4), (1, 4), (0, 1), (1, 1), (0, 0))
ROOTS = ((0, 4), (1, 4), (0, 1), (1, 1))
FIRST = (4, 3, 1)
THEN = {4: (8, 7, 5), 3: (6,), 1: (2,)}


def pick(i, values):
    n = len(values)
    total = i * 0
    for k, value in enumerate(values):
        if value:
            total = total + value * (1 - ((i + n - k) % n + n - 1) // n)
    return total


def reach(o):
    return max([o] + [reach(child) for child in PARENT if PARENT[child] == o and child <= LAST[1]])


def children(d, o):
    return [child for child in PARENT if PARENT[child] == o and child <= LAST[d]]


def remote(src, dst, ssem, rsem, dev):
    return pltpu.make_async_remote_copy(
        src_ref=src, dst_ref=dst, send_sem=ssem, recv_sem=rsem, device_id=dev, device_id_type=MESH
    )


def kernel(
    q_ref, u_ref, pk_ref, pv_ref, rk_ref, rv_ref, behav_ref, cur_ref, adv_ref, len_ref,
    gq_ref, grk_ref, grv_ref, gpk_ref, gpv_ref,
    kv, xkv, own_p, pkv, qb, ub, gb, gsend, behav, cur, adv, length_s, qt, gt, sc, dp, mx, sm, dl, dqt, dqs,
    part, rs, xself, pp, pc, pt, pz, pf,
    in_s, ag_s, ag_r, rs_s, rs_r, x_s, x_r, pm_s, pm_r, pl_s, pl_r, pa_s, pa_r, pz_s, pz_r, pf_s, pf_r,
    *, nz, nr, tok, heads, prow, full_len,
):
    hd = q_ref.shape[-1]
    scale = hd ** (-0.5)
    rows = tok * heads
    two = 2 * rows
    key_rows = 2 * tok
    shards = 2 * nr
    per_chunk = key_rows // prow
    p_chunks = shards // per_chunk

    r = lax.axis_index("resp")
    c = lax.axis_index("ctx")
    z = c // 2
    h = c % 2
    g = 1 - h
    p = 2 * r + h

    def at_z(off, col):
        return {"ctx": 2 * ((z + off + nz) % nz) + col}

    def in_plane(i):
        q = (p + i) % shards
        return q, {"resp": q // 2, "ctx": 2 * z + q % 2}

    partner = {"ctx": 2 * z + g}

    loads = [
        (rk_ref.at[g], xkv.at[pl.ds(0, tok)]),
        (rv_ref.at[g], xkv.at[pl.ds(tok, tok)]),
        (rk_ref.at[h], kv.at[z, h, pl.ds(0, tok)]),
        (rv_ref.at[h], kv.at[z, h, pl.ds(tok, tok)]),
        (pk_ref, own_p.at[pl.ds(0, prow)]),
        (pv_ref, own_p.at[pl.ds(prow, prow)]),
        (len_ref, length_s),
        (adv_ref, adv),
        (behav_ref, behav),
        (cur_ref, cur),
        (u_ref, ub),
        (q_ref.at[h], qb.at[h]),
    ]
    loads = [pltpu.make_async_copy(src, dst, in_s.at[i]) for i, (src, dst) in enumerate(loads)]
    for load in loads:
        load.start()

    barrier = pltpu.get_barrier_semaphore()
    for hop in (4, 3, 1):
        for way in (1, -1):
            pl.semaphore_signal(barrier, 1, device_id=at_z(way * hop, h), device_id_type=MESH)

    def greet(i, _):
        pl.semaphore_signal(barrier, 1, device_id=in_plane(i)[1], device_id_type=MESH)
        return 0

    lax.fori_loop(1, shards, greet, 0)
    x_kv = remote(xkv, kv.at[z, h], x_s.at[0], x_r.at[0], partner)
    x_kv_in = remote(xkv, kv.at[z, g], x_s.at[0], x_r.at[0], partner)
    x_q = remote(q_ref.at[g], qb.at[h], x_s.at[1], x_r.at[1], partner)
    x_q_in = remote(q_ref.at[g], qb.at[g], x_s.at[1], x_r.at[1], partner)
    x_g = remote(gsend, gb.at[h], x_s.at[2], x_r.at[2], partner)
    x_g_in = remote(gsend, gb.at[g], x_s.at[2], x_r.at[2], partner)

    def chunk_at(d, o):
        return (z + (2 * d - 1) * o + nz) % nz

    def edge_in(d, o, far):
        return z >= o if d == 0 else chunk_at(1, o) < far

    def edge_out(d, o, child, far):
        if d == 0:
            return jnp.logical_and(z >= o, z + child - o < nz)
        return chunk_at(1, o) < far

    def ag_out(d, o, child, blk):
        chunk = chunk_at(d, o)
        return remote(
            kv.at[chunk, blk], kv.at[chunk, blk], ag_s.at[d, child, blk], ag_r.at[d, child, blk],
            at_z((1 - 2 * d) * (child - o), h),
        )

    def ag_in(d, o, blk):
        chunk = chunk_at(d, o)
        return remote(kv.at[chunk, blk], kv.at[chunk, blk], ag_s.at[d, o, blk], ag_r.at[d, o, blk], partner)

    def ag_send(d, o, child, far, blk):
        @pl.when(edge_out(d, o, child, far))
        def _():
            ag_out(d, o, child, blk).start()

    ahead = (z - r + nz) % nz

    def pm_out(d, o, child):
        return remote(pkv.at[p], pkv.at[p], pm_s.at[d, child], pm_r.at[0], at_z((1 - 2 * d) * (child - o), h))

    def pm_at(d, o):
        return ahead == (o if d == 0 else nz - o)

    def pl_out(i):
        return remote(pkv.at[p], pkv.at[p], pl_s.at[i], pl_r.at[p], in_plane(i)[1])

    def pl_in(i):
        q, dev = in_plane(i)
        return remote(pkv.at[q], pkv.at[q], pl_s.at[i], pl_r.at[q], dev)

    def send_plane():
        def one(i, _):
            pl_out(i).start()
            return 0

        lax.fori_loop(1, shards, one, 0)

    for load in loads[:6]:
        load.wait()
    pl.semaphore_wait(barrier, 6 + shards - 1)
    x_kv.start()
    for d, o in ROOTS:
        ag_send(d, 0, o, reach(o), h)
    x_q.start()

    @pl.when(z == r)
    def _():
        pkv[p] = own_p[...]
        for o in FIRST:
            for d in range(2):
                pm_out(d, 0, o).start()

    row_of = lax.broadcasted_iota(jnp.int32, (rows, tok), 0) // heads
    col_of = lax.broadcasted_iota(jnp.int32, (rows, tok), 1)

    position = c * tok + lax.broadcasted_iota(jnp.int32, (1, tok), 1)
    for load in loads[6:]:
        load.wait()

    def weighted(member):
        length = jnp.full((1, tok), length_s[member], jnp.int32)
        ratio = jnp.minimum(jnp.exp(cur[pl.ds(member, 1), :] - behav[pl.ds(member, 1), :]), RATIO_CAP)
        valid = (position < length).astype(F32)
        weight = -adv[member] * ratio * valid * (full_len / length.astype(F32))
        spread = jnp.where(row_of == col_of, jnp.broadcast_to(weight, (rows, tok)), 0.0)
        column = jnp.sum(spread, axis=1, keepdims=True)
        return (column * ub[member].astype(F32)).astype(BF16)

    gsend[...] = weighted(g)
    x_g.start()

    @pl.when(z == r)
    def _():
        send_plane()

    gb[h] = weighted(h)
    x_kv_in.wait_recv()
    for d, o in ROOTS:
        ag_send(d, 0, o, reach(o), g)

    def ag_step(i):
        o = pick(i, ORDER)
        far = pick(i, [reach(o) if o <= LAST[1] else 0 for o in ORDER])
        far_next = pick(i, [reach(o + 1) if o + 1 in children(1, o) else 0 for o in ORDER])
        for blk in (h, g):
            for d in range(2):

                @pl.when(edge_in(d, o, far))
                def _():
                    ag_in(d, o, blk).wait_recv()

                    @pl.when(o == 4)
                    def _():
                        ag_send(d, 4, 7, reach(7), blk)

                    @pl.when(jnp.logical_and(o % 3 != 0, o < LAST[d]))
                    def _():
                        ag_send(d, o, o + 1, far_next, blk)

    def is_first():
        at = [pm_at(d, o) for d in range(2) for o in FIRST]
        return functools.reduce(jnp.logical_or, at)

    def pm_first():
        @pl.when(is_first())
        def _():
            pm_out(0, 0, 1).wait_recv()
            for d in range(2):
                for o in FIRST:

                    @pl.when(pm_at(d, o))
                    def _():
                        for child in THEN[o]:
                            if child <= LAST[d]:
                                pm_out(d, o, child).start()

            send_plane()

    def pm_then():
        @pl.when(jnp.logical_not(jnp.logical_or(is_first(), ahead == 0)))
        def _():
            pm_out(0, 0, 1).wait_recv()
            send_plane()

    def scores_of(keys, values):
        s = jnp.dot(keys, qt[...], preferred_element_type=F32) * scale
        return s, jnp.dot(values, gt[...], preferred_element_type=F32)

    def chunk_of(j, at):
        return kv[j, :, pl.ds(at, tok), :].reshape(key_rows, hd)

    def prompt_of(i, at):
        return pkv[pl.ds(i * per_chunk, per_chunk), pl.ds(at, prow), :].reshape(key_rows, hd)

    def take(j, keys, values):
        s, grad_p = scores_of(keys, values)
        sc[j] = s
        dp[j] = grad_p
        old = mx[...]
        m = jnp.maximum(old, jnp.max(s, axis=0, keepdims=True))
        e = jnp.exp(s - m)
        fix = jnp.exp(old - m)
        mx[...] = m
        sm[...] = sm[...] * fix + jnp.sum(e, axis=0, keepdims=True)
        dl[...] = dl[...] * fix + jnp.sum(e * grad_p, axis=0, keepdims=True)

    def take_pair(i):
        o = pick(i, ORDER)

        def one(d, _):
            j = chunk_at(d, o)

            @pl.when(jnp.logical_and(j < z, o + d < 9))
            def _():
                take(j, chunk_of(j, 0), chunk_of(j, tok))

            return 0

        lax.fori_loop(0, 2, one, 0)

    def early(i, _):
        ag_step(i)
        return 0

    ag_step(jnp.int32(0))
    pm_first()
    lax.fori_loop(1, 3, early, 0)
    pm_then()

    x_q_in.wait_recv()
    qt[...] = qb[...].reshape(two, hd).T
    x_g_in.wait_recv()
    gt[...] = gb[...].reshape(two, hd).T
    s, grad_p = scores_of(chunk_of(z, 0), chunk_of(z, tok))
    key_pos = lax.broadcasted_iota(jnp.int32, (key_rows, two), 0)
    row_pos = lax.broadcasted_iota(jnp.int32, (key_rows, two), 1) // heads
    s = jnp.where(key_pos <= row_pos, s, -jnp.inf)
    sc[z] = s
    dp[z] = grad_p
    m = jnp.max(s, axis=0, keepdims=True)
    e = jnp.exp(s - m)
    mx[...] = m
    sm[...] = jnp.sum(e, axis=0, keepdims=True)
    dl[...] = jnp.sum(e * grad_p, axis=0, keepdims=True)

    def behind(i, _):
        @pl.when(i > 2)
        def _():
            ag_step(i)

        take_pair(i)
        return 0

    lax.fori_loop(0, len(ORDER), behind, 0)

    def wait_plane(i, _):
        pl_in(i).wait_recv()
        return 0

    lax.fori_loop(1, shards, wait_plane, 0)

    def take_prompt(i, _):
        take(nz + i, prompt_of(i, 0), prompt_of(i, prow))
        return 0

    lax.fori_loop(0, p_chunks, take_prompt, 0)

    inv = 1.0 / sm[...]
    sm[...] = inv
    dl[...] = dl[...] * inv
    dqt[...] = jnp.zeros_like(dqt)

    def give(j, keys):
        probs = (jnp.exp(sc[j] - mx[...]) * sm[...]).astype(BF16)
        grad_s = (probs.astype(F32) * (dp[j] - dl[...])).astype(BF16)
        d_values = jnp.dot(probs, gb[...].reshape(two, hd), preferred_element_type=F32)
        d_keys = jnp.dot(grad_s, qb[...].reshape(two, hd), preferred_element_type=F32) * scale
        dqt[...] += jnp.dot(keys.T, grad_s, preferred_element_type=F32)
        return d_keys.astype(BF16), d_values.astype(BF16)

    def pa_out(i):
        q, dev = in_plane(i)
        return remote(pp.at[q], pc.at[p], pa_s.at[i], pa_r.at[p], dev)

    def pa_in(i):
        q, dev = in_plane(i)
        return remote(pp.at[q], pc.at[q], pa_s.at[i], pa_r.at[q], dev)

    def give_prompt(i, _):
        d_keys, d_values = give(nz + i, prompt_of(i, 0))
        pp[pl.ds(i * per_chunk, per_chunk), pl.ds(0, prow), :] = d_keys.reshape(per_chunk, prow, hd)
        pp[pl.ds(i * per_chunk, per_chunk), pl.ds(prow, prow), :] = d_values.reshape(per_chunk, prow, hd)
        return 0

    lax.fori_loop(0, p_chunks, give_prompt, 0)

    def send_pa(i, _):
        pa_out(i).start()
        return 0

    lax.fori_loop(1, shards, send_pa, 0)

    def give_at(d, o):
        j = chunk_at(d, o)

        @pl.when(j <= z)
        def _():
            d_keys, d_values = give(j, chunk_of(j, 0))
            part[d, o, :, pl.ds(0, tok), :] = d_keys.reshape(2, tok, hd)
            part[d, o, :, pl.ds(tok, tok), :] = d_values.reshape(2, tok, hd)

        @pl.when(j > z)
        def _():
            part[d, o] = jnp.zeros((2, 2 * tok, hd), BF16)

    def rs_out(d, o, hop, blk):
        return remote(
            part.at[d, o, blk], rs.at[d, o, blk], rs_s.at[d, o, blk], rs_r.at[d, o, blk], at_z((2 * d - 1) * hop, h)
        )

    def rs_root(d, o, col):
        return remote(
            part.at[d, o, col], rs.at[d, o, h], rs_s.at[d, o, col], rs_r.at[d, o, h], at_z((2 * d - 1) * o, col)
        )

    def rs_in(d, o, blk):
        return remote(rs.at[d, o, blk], rs.at[d, o, blk], rs_s.at[d, o, blk], rs_r.at[d, o, blk], partner)

    def stage_a(i, _):
        d = pick(i, [d for d, _ in STAGE_A])
        o = pick(i, [o for _, o in STAGE_A])
        hop = pick(i, [o - PARENT[o] for _, o in STAGE_A])
        far = pick(i, [reach(o) if d else 0 for d, o in STAGE_A])
        give_at(d, o)

        @pl.when(jnp.logical_or(jnp.logical_and(d == 0, z >= o), jnp.logical_and(d == 1, chunk_at(1, o) < far)))
        def _():
            for blk in range(2):
                rs_out(d, o, hop, blk).start()

        return 0

    lax.fori_loop(0, len(STAGE_A), stage_a, 0)

    def stage_b(i, _):
        give_at(pick(i, [d for d, _ in STAGE_B]), pick(i, [o for _, o in STAGE_B]))
        return 0

    lax.fori_loop(0, len(STAGE_B), stage_b, 0)

    def join(d, o):
        @pl.when(edge_in(d, o, reach(o)))
        def _():
            for blk in range(2):
                for child in children(d, o):

                    @pl.when(edge_out(d, o, child, reach(child)))
                    def _():
                        rs_in(d, child, blk).wait_recv()
                        part[d, o, blk] = (part[d, o, blk].astype(F32) + rs[d, child, blk].astype(F32)).astype(BF16)

                if PARENT[o]:
                    rs_out(d, o, o - PARENT[o], blk).start()
                else:
                    rs_root(d, o, blk).start()

    for d, o in STAGE_B:
        join(d, o)

    def wait_pa(i, total):
        pa_in(i).wait_recv()
        return total + pc[(p + i) % shards].astype(F32)

    pt[...] = lax.fori_loop(1, shards, wait_pa, pp[p].astype(F32))
    pz_out = remote(pt, pz.at[z], pz_s.at[0], pz_r.at[z], at_z(r - z, h))

    @pl.when(z != r)
    def _():
        pz_out.start()

    def stage_c(i, _):
        give_at(pick(i, [d for d, _ in STAGE_C]), pick(i, [o for _, o in STAGE_C]))
        return 0

    lax.fori_loop(0, len(STAGE_C), stage_c, 0)

    x_own = remote(part.at[0, 0, g], xself, x_s.at[4], x_r.at[4], partner)
    x_own.start()

    dqs[...] = (dqt[...] * scale).T.astype(BF16).reshape(2, rows, hd)
    x_dq = remote(dqs.at[g], gq_ref.at[h], x_s.at[3], x_r.at[3], partner)
    x_dq_in = remote(dqs.at[g], gq_ref.at[g], x_s.at[3], x_r.at[3], partner)
    x_dq.start()
    gq_ref[h] = dqs[h]

    for d, o in ROOTS:
        join(d, o)

    def pf_out(i):
        return remote(pf, pf, pf_s.at[i], pf_r.at[0], {"resp": (r + i) % nr})

    @pl.when(z == r)
    def _():
        def wait_pz(i, total):
            src = (z + i) % nz
            remote(pt, pz.at[src], pz_s.at[0], pz_r.at[src], partner).wait_recv()
            return total + pz[src]

        pf[...] = lax.fori_loop(1, nz, wait_pz, pt[...])

        def send_pf(i, _):
            pf_out(i).start()
            return 0

        lax.fori_loop(1, nr, send_pf, 0)

    def total_of(own, member):
        total = own.astype(F32)
        for d, o in ROOTS:
            total = total + rs[d, o, member].astype(F32)
        return total.astype(BF16)

    for member in range(2):
        for d, o in ROOTS:
            used = edge_out(d, 0, o, reach(o))

            @pl.when(used)
            def _():
                rs_in(d, o, member).wait_recv()

            @pl.when(jnp.logical_not(used))
            def _():
                rs[d, o, member] = jnp.zeros((2 * tok, hd), BF16)

    mine = total_of(part[0, 0, h], h)
    grk_ref[h] = mine[:tok]
    grv_ref[h] = mine[tok:]
    x_own.wait_recv()
    theirs = total_of(xself[...], g)
    grk_ref[g] = theirs[:tok]
    grv_ref[g] = theirs[tok:]

    for item in (x_kv, x_q, x_g, x_dq, x_own):
        item.wait_send()
    for d in range(2):
        for o in range(1, LAST[d] + 1):

            @pl.when(edge_out(d, PARENT[o], o, reach(o) if d else 0))
            def _():
                for blk in range(2):
                    ag_in(d, o, blk).wait_send()

            @pl.when(edge_in(d, o, reach(o) if d else 0))
            def _():
                for blk in range(2):
                    rs_in(d, o, blk).wait_send()


    for d in range(2):
        for o in FIRST:

            @pl.when(ahead == 0)
            def _():
                pm_out(d, 0, o).wait_send()

            @pl.when(pm_at(d, o))
            def _():
                for child in THEN[o]:
                    if child <= LAST[d]:
                        pm_out(d, o, child).wait_send()

    def sent(i, _):
        pl_out(i).wait_send()
        pa_out(i).wait_send()
        return 0

    lax.fori_loop(1, shards, sent, 0)

    x_dq_in.wait_recv()

    @pl.when(z != r)
    def _():
        pz_out.wait_send()
        pf_out(0).wait_recv()

    @pl.when(z == r)
    def _():
        def sent_pf(i, _):
            pf_out(i).wait_send()
            return 0

        lax.fori_loop(1, nr, sent_pf, 0)

    gpk_ref[...] = pf[:prow]
    gpv_ref[...] = pf[prow:]


def write_out(*refs):
    n = len(refs) // 2
    sems = refs[-1]
    copies = [pltpu.make_async_copy(refs[i], refs[n + i], sems.at[i]) for i in range(n)]
    for copy in copies:
        copy.start()
    for copy in copies:
        copy.wait()


def per_device(queries, prompt_keys, prompt_values, resp_keys, resp_values, upstream, behav_logp, cur_logp, advantages, lengths):
    members, tok, heads, hd = queries.shape
    nc = lax.axis_size("ctx")
    nr = lax.axis_size("resp")
    nz = nc // 2
    prow = prompt_keys.shape[0]
    rows = tok * heads
    two = 2 * rows
    key_rows = 2 * tok
    shards = 2 * nr
    slots = nz + (nc * prow) // key_rows
    vmem = pl.BlockSpec(memory_space=pltpu.VMEM)
    hbm = pl.BlockSpec(memory_space=pltpu.HBM)
    dma = pltpu.SemaphoreType.DMA
    offs = max(LAST) + 1
    shapes = (
        jax.ShapeDtypeStruct((members, rows, hd), BF16),
        jax.ShapeDtypeStruct((members, tok, hd), BF16),
        jax.ShapeDtypeStruct((members, tok, hd), BF16),
        jax.ShapeDtypeStruct((prow, hd), F32),
        jax.ShapeDtypeStruct((prow, hd), F32),
    )
    outs = pl.pallas_call(
        functools.partial(kernel, nz=nz, nr=nr, tok=tok, heads=heads, prow=prow, full_len=tok * nc),
        name="grpo_backward",
        out_shape=shapes,
        in_specs=[hbm] * 10,
        out_specs=(vmem,) * 5,
        scratch_shapes=[
            pltpu.VMEM((nz, 2, 2 * tok, hd), BF16),
            pltpu.VMEM((2 * tok, hd), BF16),
            pltpu.VMEM((2 * prow, hd), BF16),
            pltpu.VMEM((shards, 2 * prow, hd), BF16),
            pltpu.VMEM((2, rows, hd), BF16),
            pltpu.VMEM((2, rows, hd), BF16),
            pltpu.VMEM((2, rows, hd), BF16),
            pltpu.VMEM((rows, hd), BF16),
            pltpu.VMEM((members, tok), F32),
            pltpu.VMEM((members, tok), F32),
            pltpu.SMEM((members,), F32),
            pltpu.SMEM((members,), jnp.int32),
            pltpu.VMEM((hd, two), BF16),
            pltpu.VMEM((hd, two), BF16),
            pltpu.VMEM((slots, key_rows, two), F32),
            pltpu.VMEM((slots, key_rows, two), F32),
            pltpu.VMEM((1, two), F32),
            pltpu.VMEM((1, two), F32),
            pltpu.VMEM((1, two), F32),
            pltpu.VMEM((hd, two), F32),
            pltpu.VMEM((2, rows, hd), BF16),
            pltpu.VMEM((2, offs, 2, 2 * tok, hd), BF16),
            pltpu.VMEM((2, offs, 2, 2 * tok, hd), BF16),
            pltpu.VMEM((2 * tok, hd), BF16),
            pltpu.VMEM((shards, 2 * prow, hd), BF16),
            pltpu.VMEM((shards, 2 * prow, hd), BF16),
            pltpu.VMEM((2 * prow, hd), F32),
            pltpu.VMEM((nz, 2 * prow, hd), F32),
            pltpu.VMEM((2 * prow, hd), F32),
            dma((12,)),
            dma((2, offs, 2)),
            dma((2, offs, 2)),
            dma((2, offs, 2)),
            dma((2, offs, 2)),
            dma((5,)),
            dma((5,)),
            dma((2, offs)),
            dma((1,)),
            dma((shards,)),
            dma((shards,)),
            dma((shards,)),
            dma((shards,)),
            dma((1,)),
            dma((nz,)),
            dma((nr,)),
            dma((1,)),
        ],
        compiler_params=pltpu.CompilerParams(
            collective_id=0, has_side_effects=True, vmem_limit_bytes=VMEM_BYTES
        ),
    )(
        queries.reshape(members, rows, hd),
        upstream.reshape(members, rows, hd),
        prompt_keys, prompt_values, resp_keys, resp_values, behav_logp, cur_logp, advantages, lengths,
    )
    outs = (outs[0].reshape(queries.shape), *outs[1:])
    return pl.pallas_call(
        write_out,
        name="write_out",
        out_shape=tuple(jax.ShapeDtypeStruct(o.shape, o.dtype) for o in outs),
        in_specs=[vmem] * 5,
        out_specs=(hbm,) * 5,
        scratch_shapes=[dma((5,))],
        compiler_params=pltpu.CompilerParams(vmem_limit_bytes=VMEM_BYTES),
    )(*outs)


def solution(mesh):
    placed = (
        P("resp", "ctx", None, None),
        P("ctx", None),
        P("ctx", None),
        P("resp", "ctx", None),
        P("resp", "ctx", None),
        P("resp", "ctx", None, None),
        P("resp", "ctx"),
        P("resp", "ctx"),
        P("resp"),
        P("resp"),
    )
    return jax.shard_map(
        per_device,
        mesh=mesh,
        in_specs=placed,
        out_specs=(
            P("resp", "ctx", None, None),
            P("resp", "ctx", None),
            P("resp", "ctx", None),
            P("ctx", None),
            P("ctx", None),
        ),
        check_vma=False,
    )
```
